128 devices in a mesh: frame: 16 (over y_lo, z, core), row: 8 (over y_hi, x).
Axes of the slice: x: 4, y: 4 (y_hi: 2, y_lo: 2; y = y_hi * 2 + y_lo), z: 4, core: 2. Of those that a mesh axis runs over, the one named last changes fastest.
Arguments:
- video: bfloat16 [32, 16, 128, 384], P('frame', 'row'), may hold values from -30 to 30
- down_weight: bfloat16 [1152, 384], replicated, may hold values from -0.1875 to 0.1875
- conv_weight: bfloat16 [10368, 384], P(('frame', 'row')), may hold values from -0.0625 to 0.0625
- norm_gain_vector: float32 [384], replicated, may hold values from 0.1 to 1.9
- norm_shift_vector: float32 [384], replicated, may hold values from -3 to 3
- output_gradient: bfloat16 [16, 16, 128, 384], P(None, 'row', 'frame'), may hold values from -6 to 6
Outputs:
- encoded_code: bfloat16 [16, 16, 128, 384], P(None, 'row', 'frame')
- grad_video: bfloat16 [32, 16, 128, 384], P('frame', 'row')
- grad_conv: float32 [10368, 384], P(('frame', 'row'))
- grad_down: float32 [1152, 384], P(('frame', 'row'))
- gain_gradient: float32 [384], replicated
- grad_shift: float32 [384], replicated
The draws below stay inside these ranges and needn't reach their ends.
All inputs are finite; a program needn't handle non-finite values.
Results may differ from the reference program's by a relative error of at most 0.004.
The reference program's roundings to bfloat16 on the way count: a program that leaves them out, or rounds other values in their place, can miss the bound.
Values may be sent and summed in bfloat16 or wider, within the bound.
A program may use at most 128 MiB of HBM per device.

```python
import jax
import jax.numpy as jnp
from jax import lax

C = 384
CLUSTER_TALLY = 32
T_IN = 32
T_OUT = 16
H = 16
W = 128


def draw_video(key, part):
    key = jax.random.fold_in(key, 11)
    first, second, third = jax.random.split(key, 3)
    array_dimensions = (T_IN, H, W, C)
    base = jnp.clip(jax.random.normal(first, array_dimensions, jnp.float32), -6.0, 6.0)
    scales = 0.5 + jax.random.uniform(second, (C,), jnp.float32)
    offsets = jnp.clip(0.3 * jax.random.normal(third, (C,), jnp.float32), -1.0, 1.0)
    position = jnp.arange(H, dtype=jnp.float32) / max(H - 1, 1)
    rising = jnp.exp(jnp.log(3.0) * position)[None, :, None, None]
    return ((base * scales + offsets) * rising).astype(jnp.bfloat16)


def block_levels(stream_key, shape, pieces, least, high):
    factor_of = 1.0
    for dim, parts in pieces:
        steps = jax.random.uniform(jax.random.fold_in(jax.random.fold_in(stream_key, 6), dim), (parts,), jnp.float32, least / len(pieces), high / len(pieces))
        factor_of = factor_of * jnp.repeat(jnp.exp(steps), shape[dim] // parts).reshape((-1,) + (1,) * (len(shape) - 1 - dim))
    return factor_of


def gaussian(rng, shape, scale, reach, pieces=(), kind=jnp.bfloat16):
    values = scale * jax.random.normal(rng, shape, jnp.float32)
    if pieces:
        values = values * block_levels(rng, shape, pieces, -0.22, 0.18)
    return jnp.clip(values, -reach, reach).astype(kind)


def setup_inputs(seed: int = 0) -> dict:
    splits = jax.random.split(jax.random.key(seed), 7)
    return {
        "video": draw_video(jax.random.fold_in(splits[6], 71), 0),
        "down_weight": gaussian(splits[1], (3 * C, C), (3 * C) ** -0.5, 0.1875),
        "conv_weight": gaussian(splits[2], (27 * C, C), (27 * C) ** -0.5, 0.0625, ((0, 128),)),
        "norm_gain_vector": jnp.clip(1.0 + 0.18 * jax.random.normal(splits[3], (C,), jnp.float32), 0.1, 1.9),
        "norm_shift_vector": gaussian(splits[4], (C,), 0.5, 3.0, (), jnp.float32),
        "output_gradient": gaussian(splits[5], (T_OUT, H, W, C), 1.0, 6.0, ((1, 8), (2, 16))),
    }


def swish_derivative(before_nonlinearity):
    sigma = jax.nn.sigmoid(before_nonlinearity)
    return sigma * (1.0 + before_nonlinearity * (1.0 - sigma))

def contract_rows(left, right):
    return lax.dot_general(left, right, (((0,), (0,)), ((), ())), preferred_element_type=jnp.float32)

def contract_cols(left, right):
    return lax.dot_general(left, right, (((1,), (1,)), ((), ())), preferred_element_type=jnp.float32)

def reference(video, down_weight, conv_weight, norm_gain_vector, norm_shift_vector, output_gradient):
    t_in, height, width, chans = video.shape
    t_out = t_in // 2
    cluster_width = chans // CLUSTER_TALLY
    zero_frame = jnp.zeros((1, height, width, chans), video.dtype)
    before = jnp.concatenate([zero_frame, video[1:-1:2]], 0).reshape(-1, chans)
    even_frames = video[0::2].reshape(-1, chans)
    odd_frames = video[1::2].reshape(-1, chans)
    inputs = [before, even_frames, odd_frames]
    down_wide = jnp.zeros((t_out * height * width, chans), jnp.float32)
    for k in range(3):
        down_wide = down_wide + jnp.dot(inputs[k], down_weight[k * chans:(k + 1) * chans], preferred_element_type=jnp.float32)
    halved_clip = down_wide.astype(jnp.bfloat16).reshape(t_out, height, width, chans)
    halve_frames_routine = halved_clip.astype(jnp.float32)
    element_tally = t_out * height * width * cluster_width
    cluster_average = lax.optimization_barrier(jnp.sum(halve_frames_routine, (0, 1, 2))).reshape(CLUSTER_TALLY, cluster_width).sum(1) / element_tally
    cluster_squares = lax.optimization_barrier(jnp.sum(halve_frames_routine * halve_frames_routine, (0, 1, 2))).reshape(CLUSTER_TALLY, cluster_width).sum(1) / element_tally
    rstd_group = lax.rsqrt(cluster_squares - cluster_average * cluster_average + 1e-06)
    feature_average = jnp.repeat(cluster_average, cluster_width)
    feature_reciprocal_spread = jnp.repeat(rstd_group, cluster_width)
    standardized_source = (halve_frames_routine - feature_average) * feature_reciprocal_spread
    before_nonlinearity = standardized_source * norm_gain_vector + norm_shift_vector
    act = jax.nn.silu(before_nonlinearity).astype(jnp.bfloat16)
    act_pad = jnp.pad(act, ((2, 0), (1, 1), (1, 1), (0, 0)))
    grad_pad = jnp.pad(output_gradient, ((0, 2), (1, 1), (1, 1), (0, 0)))
    grad_flat = output_gradient.reshape(-1, chans)
    residual_path = jnp.zeros((t_out * height * width, chans), jnp.float32)
    activation_cotangent = jnp.zeros((t_out * height * width, chans), jnp.float32)
    blocks = []
    for a in range(3):
        for b in range(3):
            for e in range(3):
                k = 9 * a + 3 * b + e
                kernel = conv_weight[k * chans:(k + 1) * chans]
                tap_rows = act_pad[a:a + t_out, b:b + height, e:e + width].reshape(-1, chans)
                residual_path = residual_path + jnp.dot(tap_rows, kernel, preferred_element_type=jnp.float32)
                blocks.append(contract_rows(tap_rows, grad_flat))
                grad_rows = grad_pad[2 - a:2 - a + t_out, 2 - b:2 - b + height, 2 - e:2 - e + width].reshape(-1, chans)
                activation_cotangent = activation_cotangent + contract_cols(grad_rows, kernel)
    encoded_code = (halve_frames_routine + residual_path.reshape(halve_frames_routine.shape)).astype(jnp.bfloat16)
    grad_conv = jnp.concatenate(blocks, 0)
    before_nonlinearity_cotangent = activation_cotangent.reshape(halve_frames_routine.shape) * swish_derivative(before_nonlinearity)
    grad_shift = lax.optimization_barrier(jnp.sum(before_nonlinearity_cotangent, (0, 1, 2)))
    gain_gradient = lax.optimization_barrier(jnp.sum(before_nonlinearity_cotangent * standardized_source, (0, 1, 2)))
    first_moment_mean = jnp.repeat((norm_gain_vector * grad_shift).reshape(CLUSTER_TALLY, cluster_width).sum(1) / element_tally, cluster_width)
    second_moment_mean = jnp.repeat((norm_gain_vector * gain_gradient).reshape(CLUSTER_TALLY, cluster_width).sum(1) / element_tally, cluster_width)
    latent_gradient = (output_gradient.astype(jnp.float32) + feature_reciprocal_spread * (before_nonlinearity_cotangent * norm_gain_vector - first_moment_mean - standardized_source * second_moment_mean)).astype(jnp.bfloat16)
    latent_flat = latent_gradient.reshape(-1, chans)
    next_flat = jnp.concatenate([latent_gradient[1:], jnp.zeros((1, height, width, chans), jnp.bfloat16)], 0).reshape(-1, chans)
    even_grad = contract_cols(latent_flat, down_weight[chans:2 * chans])
    odd_grad = contract_cols(latent_flat, down_weight[2 * chans:]) + contract_cols(next_flat, down_weight[:chans])
    grad_video = jnp.stack([even_grad.reshape(t_out, height, width, chans), odd_grad.reshape(t_out, height, width, chans)], 1)
    grad_video = grad_video.reshape(t_in, height, width, chans).astype(jnp.bfloat16)
    grad_down = jnp.concatenate([contract_rows(inputs[k], latent_flat) for k in range(3)], 0)
    return (encoded_code, grad_video, grad_conv, grad_down, gain_gradient, grad_shift)
```

```python
import functools
import jax
import jax.numpy as jnp
from jax import lax
from jax.experimental import pallas as pl
from jax.experimental.pallas import tpu as pltpu
from jax.sharding import PartitionSpec as P

MESH = pl.DeviceIdType.MESH
AXES = "xyz"
ORDERS = ("xyz", "yzx", "zxy")
BLOCK = 96
LANES = 128


def position():
    f, r = lax.axis_index("frame"), lax.axis_index("row")
    y = lax.div(r, 4) * 2 + lax.div(f, 8)
    pos = {"x": lax.rem(r, 4), "y": y, "z": lax.rem(lax.div(f, 2), 4)}
    return f, r, pos, lax.rem(f, 2)


def device_at(pos, core):
    frame = lax.rem(pos["y"], 2) * 8 + pos["z"] * 2 + core
    row = lax.div(pos["y"], 2) * 4 + pos["x"]
    return (frame, row)


def shifted(pos, axis, steps):
    moved = dict(pos)
    moved[axis] = lax.rem(pos[axis] + (steps + 4), 4)
    return moved


def chip_neighbours(pos, core):
    near = [device_at(shifted(pos, axis, s), core) for axis in AXES for s in (1, -1)]
    return near + [device_at(pos, 1 - core)]


def greet(devices):
    barrier = pltpu.get_barrier_semaphore()
    for device in devices:
        pl.semaphore_signal(barrier, inc=1, device_id=device, device_id_type=MESH)
    pl.semaphore_wait(barrier, len(devices))


def remote(src, dst, sems, index, device):
    return pltpu.make_async_remote_copy(
        src_ref=src,
        dst_ref=dst,
        send_sem=sems[0].at[index],
        recv_sem=sems[1].at[index],
        device_id=device,
        device_id_type=MESH,
    )


GATHER_COPIES = 16


def gather_steps(pos, core, order, buf, sems, base):
    a, b, c = order
    ca, cb, cc = pos[a], pos[b], pos[c]
    sent = []

    def start(src, dst, device):
        op = remote(src, dst, sems, base + len(sent), device)
        op.start()
        sent.append(op)
        return op

    whole = {
        c: lambda i: buf.at[core, ca, cb, i],
        b: lambda i: buf.at[core, ca, i],
        a: lambda i: buf.at[core, i],
    }
    half = BLOCK // 2
    parts = {
        c: lambda i, h: buf.at[core, ca, cb, i, pl.ds(h * half, half)],
        b: lambda i, h: buf.at[core, ca, i, pl.ds(2 * h, 2)],
        a: lambda i, h: buf.at[core, i, pl.ds(2 * h, 2)],
    }
    other = device_at(pos, 1 - core)
    for axis in (c, b, a):
        me = pos[axis]
        up, down = shifted(pos, axis, 1), shifted(pos, axis, -1)
        mine, one, ref = whole[axis](me), whole[axis], parts[axis]
        first = start(mine, mine, device_at(up, core))
        second = start(mine, mine, device_at(down, core))
        if axis == a:
            start(mine, mine, other)
        yield
        first.wait_recv()
        third = start(ref(down[axis], 0), ref(down[axis], 0), device_at(up, core))
        if axis == a:
            start(one(down[axis]), one(down[axis]), other)
        second.wait_recv()
        fourth = start(ref(up[axis], 1), ref(up[axis], 1), device_at(down, core))
        if axis == a:
            start(one(up[axis]), one(up[axis]), other)
        yield
        third.wait_recv()
        fourth.wait_recv()
    far = shifted(pos, a, 2)[a]
    start(buf.at[core, far], buf.at[core, far], other)
    yield
    for k, op in enumerate(sent):
        if k in (10, 12, 14, 15):
            op.wait_recv()
        op.wait_send()


def interleave(steps):
    steps = list(steps)
    while steps:
        left = []
        for step in steps:
            try:
                next(step)
                left.append(step)
            except StopIteration:
                pass
        steps = left


def static_place(d, order):
    x, y_hi, core = d % 4, (d // 4) % 2, (d // 8) % 2
    return core, x, y_hi


def gather_kernel(w_ref, out_ref, b0, b1, b2, wide, send, recv):
    f, r, pos, core = position()
    bufs = (b0, b1, b2)
    greet(chip_neighbours(pos, core))
    for j, order in enumerate(ORDERS):
        a, b, c = order
        bufs[j][core, pos[a], pos[b], pos[c]] = w_ref[j]
    interleave(
        gather_steps(pos, core, order, bufs[j], (send, recv), j * GATHER_COPIES)
        for j, order in enumerate(ORDERS)
    )

    def unpack(g, _):
        y_lo, z = lax.div(g, 4), lax.rem(g, 4)
        for i in range(16):
            at = {"x": i % 4, "y": 2 * ((i // 4) % 2) + y_lo, "z": z}
            for j, (a, b, c) in enumerate(ORDERS):
                block = bufs[j][i // 8, at[a], at[b], at[c]].astype(jnp.float32)
                wide[81 * i : 81 * i + 81, LANES * j : LANES * (j + 1)] = block[:81]
        out_ref[pl.ds(pl.multiple_of(g * 1296, 16), 1296)] = wide[...].astype(jnp.bfloat16)
        return 0

    lax.fori_loop(0, 8, unpack, 0)


def gather_weights(w):
    padded = jnp.pad(w, ((0, BLOCK - w.shape[0]), (0, 0)))
    split = padded.reshape(BLOCK, 3, LANES).transpose(1, 0, 2)
    buf = pltpu.VMEM((2, 4, 4, 4, BLOCK, LANES), jnp.bfloat16)
    return pl.pallas_call(
        gather_kernel,
        out_shape=jax.ShapeDtypeStruct((10368, 384), jnp.bfloat16),
        in_specs=[pl.BlockSpec(memory_space=pltpu.VMEM)],
        out_specs=pl.BlockSpec(memory_space=pltpu.VMEM),
        scratch_shapes=[buf, buf, buf, pltpu.VMEM((1296, 384), jnp.float32),
                        pltpu.SemaphoreType.DMA((3 * GATHER_COPIES,)),
                        pltpu.SemaphoreType.DMA((3 * GATHER_COPIES,))],
        compiler_params=pltpu.CompilerParams(
            collective_id=0, has_side_effects=True, vmem_limit_bytes=60 * 2**20),
    )(split)


SCATTER_COPIES = 16


def add_into(count, target, terms):
    def step(i, _):
        total = terms[0](i).astype(jnp.float32)
        for term in terms[1:]:
            total = total + term(i).astype(jnp.float32)
        target(i, total)
        return 0

    lax.fori_loop(0, count, step, 0)


def scatter_steps(pos, core, order, rows, piles, got, near, q, near_q, u, near_u, sems, base, out):
    a, b, c = order
    ca, cb, cc = pos[a], pos[b], pos[c]
    half = rows // 2
    sent = []

    def start(src, dst, device):
        op = remote(src, dst, sems, base + len(sent), device)
        op.start()
        sent.append(op)
        return op

    def toward(axis, steps):
        return device_at(shifted(pos, axis, steps), core)

    def at(axis, steps):
        return shifted(pos, axis, steps)[axis]

    other = device_at(pos, 1 - core)
    far, up, down = at(a, 2), at(a, 1), at(a, -1)
    swaps = [start(piles.at[1 - core, i], got.at[i], other) for i in (far, up, down, ca)]
    yield

    def store(i):
        def put(k, total):
            piles[core, i, k] = total.astype(jnp.bfloat16)
        return put

    def pair(i, first=0):
        return [lambda k: piles[core, i, k + first], lambda k: got[i, k + first]]

    near_a, near_b, near_c, near_d = near
    swaps[0].wait_recv()
    add_into(4, store(far), pair(far))
    op_a = start(piles.at[core, far, pl.ds(0, 2)], near_a, toward(a, 1))
    op_b = start(piles.at[core, far, pl.ds(2, 2)], near_b, toward(a, -1))
    yield
    swaps[1].wait_recv()
    op_a.wait_recv()
    add_into(2, store(up), pair(up) + [lambda k: near_a[k]])
    add_into(2, lambda k, total: store(up)(k + 2, total), pair(up, 2))
    op_c = start(piles.at[core, up], near_c, toward(a, 1))
    swaps[2].wait_recv()
    op_b.wait_recv()
    add_into(2, store(down), pair(down))
    add_into(2, lambda k, total: store(down)(k + 2, total), pair(down, 2) + [lambda k: near_b[k]])
    op_d = start(piles.at[core, down], near_d, toward(a, -1))
    yield
    swaps[3].wait_recv()
    op_c.wait_recv()
    op_d.wait_recv()

    def put_q(k, total):
        q[k] = total

    add_into(4, put_q, pair(ca) + [lambda k: near_c[k], lambda k: near_d[k]])
    for axis, v, near_v, low, high, lower, upper in (
        (b, q, near_q, lambda i: q.at[i, pl.ds(0, 2)], lambda i: q.at[i, pl.ds(2, 2)],
         pl.ds(0, 2), pl.ds(2, 2)),
        (c, u, near_u, lambda i: u.at[i, pl.ds(0, half)], lambda i: u.at[i, pl.ds(half, half)],
         pl.ds(0, half), pl.ds(half, half)),
    ):
        far, up, down, me = at(axis, 2), at(axis, 1), at(axis, -1), pos[axis]
        near_a, near_b, near_c, near_d = near_v
        op_a = start(low(far), near_a, toward(axis, 1))
        op_b = start(high(far), near_b, toward(axis, -1))
        yield
        op_a.wait_recv()
        v[up, lower] = v[up, lower] + near_a[...]
        op_c = start(v.at[up], near_c, toward(axis, 1))
        op_b.wait_recv()
        v[down, upper] = v[down, upper] + near_b[...]
        op_d = start(v.at[down], near_d, toward(axis, -1))
        yield
        op_c.wait_recv()
        op_d.wait_recv()
        total = v[me] + near_c[...] + near_d[...]
        if axis == b:
            u[...] = total
        else:
            out(total)
    yield
    for op in sent:
        op.wait_send()


def scatter_scratch(rows):
    def bf(*lead):
        return pltpu.VMEM(lead + (rows, LANES), jnp.bfloat16)

    def f32(*lead):
        return pltpu.VMEM(lead + (rows, LANES), jnp.float32)

    half = pltpu.VMEM((rows // 2, LANES), jnp.float32)
    one = [bf(2, 4, 4, 4), bf(4, 4, 4), bf(2, 4), bf(2, 4), bf(4, 4), bf(4, 4), f32(4, 4),
           f32(2), f32(2), f32(4), f32(4), f32(4), half, half, f32(), f32()]
    return one


def scatter_kernel(rows, gc_ref, gd_ref, out_ref, *scratch):
    f, r, pos, core = position()
    size = (len(scratch) - 2) // 3
    sets = [scratch[j * size : (j + 1) * size] for j in range(3)]
    send, recv = scratch[-2:]
    greet(chip_neighbours(pos, core))

    def pack(g, _):
        y_lo, z = lax.div(g, 4), lax.rem(g, 4)
        wide = gc_ref.at[pl.ds(pl.multiple_of(g * 1296, 16), 1296)]
        thin = gd_ref.at[pl.ds(pl.multiple_of(g * 144, 16), 144)]
        for i in range(16):
            at = {"x": i % 4, "y": 2 * ((i // 4) % 2) + y_lo, "z": z}
            for j, (a, b, c) in enumerate(ORDERS):
                cols = slice(LANES * j, LANES * (j + 1))
                block = jnp.concatenate(
                    [wide[81 * i : 81 * i + 81, cols], thin[9 * i : 9 * i + 9, cols],
                     jnp.zeros((6, LANES), jnp.float32)], 0)
                sets[j][0][i // 8, at[a], at[b], at[c]] = block.astype(jnp.bfloat16)
        return 0

    lax.fori_loop(0, 8, pack, 0)

    def run(j, order):
        s = sets[j]

        def out(total):
            out_ref[:, LANES * j : LANES * (j + 1)] = total

        return scatter_steps(pos, core, order, rows, s[0], s[1], s[2:6], s[6], s[7:11],
                             s[11], s[12:16], (send, recv), j * SCATTER_COPIES, out)

    interleave(run(j, order) for j, order in enumerate(ORDERS))


def scatter_sum(gc, gd):
    vmem = pl.BlockSpec(memory_space=pltpu.VMEM)
    return pl.pallas_call(
        functools.partial(scatter_kernel, BLOCK),
        out_shape=jax.ShapeDtypeStruct((BLOCK, 384), jnp.float32),
        in_specs=[vmem, vmem],
        out_specs=vmem,
        scratch_shapes=scatter_scratch(BLOCK) * 3 + [
            pltpu.SemaphoreType.DMA((3 * SCATTER_COPIES,)),
            pltpu.SemaphoreType.DMA((3 * SCATTER_COPIES,))],
        compiler_params=pltpu.CompilerParams(
            collective_id=1, has_side_effects=True, vmem_limit_bytes=60 * 2**20),
    )(gc, gd)


def sum_steps(f, r, x_ref, out_ref, row_in, frame_in, row_total, sems, base=0):
    row_in[r] = x_ref[...]
    ops = []
    for s in range(1, 8):
        peer = lax.rem(r + s, 8)
        op = remote(row_in.at[r], row_in.at[r], sems, base + s - 1, (f, peer))
        op.start()
        ops.append(op)
    yield
    for op in ops:
        op.wait_recv()
    total = row_in[0]
    for s in range(1, 8):
        total = total + row_in[s]
    frame_in[f] = total
    more = []
    for s in range(1, 16):
        peer = lax.rem(f + s, 16)
        op = remote(frame_in.at[f], frame_in.at[f], sems, base + 6 + s, (peer, r))
        op.start()
        more.append(op)
    yield
    for op in more:
        op.wait_recv()
    total = frame_in[0]
    for s in range(1, 16):
        total = total + frame_in[s]
    out_ref[...] = total
    for op in ops + more:
        op.wait_send()


def sum_kernel(x_ref, out_ref, row_in, frame_in, send, recv):
    f, r = lax.axis_index("frame"), lax.axis_index("row")
    greet([(f, lax.rem(r + s, 8)) for s in range(1, 8)]
          + [(lax.rem(f + s, 16), r) for s in range(1, 16)])
    interleave([sum_steps(f, r, x_ref, out_ref, row_in, frame_in, None, (send, recv))])


def all_sum(x):
    vmem = pl.BlockSpec(memory_space=pltpu.VMEM)
    return pl.pallas_call(
        sum_kernel,
        out_shape=jax.ShapeDtypeStruct((8, 384), jnp.float32),
        in_specs=[vmem],
        out_specs=vmem,
        scratch_shapes=[pltpu.VMEM((8, 8, 384), jnp.float32), pltpu.VMEM((16, 8, 384), jnp.float32),
                        pltpu.SemaphoreType.DMA((22,)), pltpu.SemaphoreType.DMA((22,))],
        compiler_params=pltpu.CompilerParams(collective_id=2, has_side_effects=True),
    )(x)


CLUSTER_TALLY = 32


def from_behind(value, axis, steps):
    count = lax.axis_size(axis)
    first, last = (max(0, -steps), min(count, count - steps))
    return lax.ppermute(value, axis, [(source, source + steps) for source in range(first, last)])


def extended(block, sides, width):
    for axis, dim in sides:
        count = lax.axis_size(axis)
        forward = [(i, i + 1) for i in range(count - 1)]
        backward = [(target, source) for source, target in forward]
        low = lax.ppermute(
            lax.slice_in_dim(block, block.shape[dim] - width, None, axis=dim), axis, forward
        )
        high = lax.ppermute(lax.slice_in_dim(block, 0, width, axis=dim), axis, backward)
        block = jnp.concatenate([low, block, high], axis=dim)
    return block


def swish_derivative(before_nonlinearity):
    sigma = jax.nn.sigmoid(before_nonlinearity)
    return sigma * (1.0 + before_nonlinearity * (1.0 - sigma))


def contract_rows(left, right):
    return lax.dot_general(
        left, right, (((0,), (0,)), ((), ())), preferred_element_type=jnp.float32
    )


def contract_cols(left, right):
    return lax.dot_general(
        left, right, (((1,), (1,)), ((), ())), preferred_element_type=jnp.float32
    )


def forward_taps(padded, frames, height, width):
    pieces = []
    for a in range(3):
        for b in range(3):
            for e in range(3):
                pieces.append(padded[a : a + frames, b : b + height, e : e + width])
    joined = jnp.concatenate(pieces, -1)
    return joined.reshape(-1, joined.shape[-1])


def backward_taps(padded, frames, height, width):
    pieces = []
    for a in range(3):
        for b in range(3):
            for e in range(3):
                pieces.append(
                    padded[2 - a : 2 - a + frames, 2 - b : 2 - b + height, 2 - e : 2 - e + width]
                )
    joined = jnp.concatenate(pieces, -1)
    return joined.reshape(-1, joined.shape[-1])


def pair_sum(first, second):
    rows = jnp.concatenate([first[None], second[None], jnp.zeros((6, 384), jnp.float32)], 0)
    total = all_sum(rows)
    return total[0], total[1]


def body(video, down_weight, conv_weight, norm_gain_vector, norm_shift_vector, output_gradient):
    chans = video.shape[3]
    cluster_width = chans // CLUSTER_TALLY
    frame_count = lax.axis_size("frame")
    row_count = lax.axis_size("row")
    devices = frame_count * row_count
    kernel_full = gather_weights(conv_weight)
    before = from_behind(video[1:2], "frame", 1)
    stacked = jnp.concatenate([before[0], video[0], video[1]], -1)
    slab_rows, slab_cols = (stacked.shape[0], stacked.shape[1])
    flat_in = stacked.reshape(-1, 3 * chans)
    down_frame = jnp.dot(flat_in, down_weight, preferred_element_type=jnp.float32)
    down_frame = down_frame.astype(jnp.bfloat16).reshape(1, slab_rows, slab_cols, chans)
    halved_clip = lax.all_to_all(down_frame, "frame", split_axis=2, concat_axis=0, tiled=True)
    halve_frames_routine = halved_clip.astype(jnp.float32)
    frames, height, width = (halved_clip.shape[0], halved_clip.shape[1], halved_clip.shape[2])
    total_sum, total_square = pair_sum(
        jnp.sum(halve_frames_routine, (0, 1, 2)),
        jnp.sum(halve_frames_routine * halve_frames_routine, (0, 1, 2)),
    )
    element_tally = frames * height * width * devices * cluster_width
    cluster_average = total_sum.reshape(CLUSTER_TALLY, cluster_width).sum(1) / element_tally
    cluster_squares = total_square.reshape(CLUSTER_TALLY, cluster_width).sum(1) / element_tally
    rstd_group = lax.rsqrt(cluster_squares - cluster_average * cluster_average + 1e-06)
    feature_average = jnp.repeat(cluster_average, cluster_width)
    feature_reciprocal_spread = jnp.repeat(rstd_group, cluster_width)
    standardized_source = (halve_frames_routine - feature_average) * feature_reciprocal_spread
    before_nonlinearity = standardized_source * norm_gain_vector + norm_shift_vector
    act = jax.nn.silu(before_nonlinearity).astype(jnp.bfloat16)
    bordered = extended(act, (("frame", 2), ("row", 1)), 1)
    padded = jnp.pad(bordered, ((2, 0), (0, 0), (0, 0), (0, 0)))
    tap_rows = forward_taps(padded, frames, height, width)
    residual_path = jnp.dot(tap_rows, kernel_full, preferred_element_type=jnp.float32).reshape(
        halve_frames_routine.shape
    )
    encoded_local = (halve_frames_routine + residual_path).astype(jnp.bfloat16)
    grad_flat = output_gradient.reshape(-1, chans)
    piece = tap_rows
    conv_part = contract_rows(piece, grad_flat)
    grad_border = extended(output_gradient, (("frame", 2), ("row", 1)), 1)
    grad_padded = jnp.pad(grad_border, ((0, 2), (0, 0), (0, 0), (0, 0)))
    flipped = kernel_full.reshape(27, chans, chans).transpose(0, 2, 1).reshape(27 * chans, chans)
    activation_cotangent = jnp.dot(
        backward_taps(grad_padded, frames, height, width),
        flipped,
        preferred_element_type=jnp.float32,
    )
    before_nonlinearity_cotangent = activation_cotangent.reshape(
        halve_frames_routine.shape
    ) * swish_derivative(before_nonlinearity)
    grad_shift, gain_gradient = pair_sum(
        jnp.sum(before_nonlinearity_cotangent, (0, 1, 2)),
        jnp.sum(before_nonlinearity_cotangent * standardized_source, (0, 1, 2)),
    )
    first_moment_mean = jnp.repeat(
        (norm_gain_vector * grad_shift).reshape(CLUSTER_TALLY, cluster_width).sum(1)
        / element_tally,
        cluster_width,
    )
    second_moment_mean = jnp.repeat(
        (norm_gain_vector * gain_gradient).reshape(CLUSTER_TALLY, cluster_width).sum(1)
        / element_tally,
        cluster_width,
    )
    latent_gradient = (
        output_gradient.astype(jnp.float32)
        + feature_reciprocal_spread
        * (
            before_nonlinearity_cotangent * norm_gain_vector
            - first_moment_mean
            - standardized_source * second_moment_mean
        )
    ).astype(jnp.bfloat16)
    latent_grad = lax.all_to_all(latent_gradient, "frame", split_axis=0, concat_axis=2, tiled=True)
    next_grad = from_behind(latent_grad, "frame", -1)
    latent_flat = latent_grad.reshape(-1, chans)
    next_flat = next_grad.reshape(-1, chans)
    even_grad = contract_cols(latent_flat, down_weight[chans : 2 * chans])
    odd_grad = contract_cols(latent_flat, down_weight[2 * chans :]) + contract_cols(
        next_flat, down_weight[:chans]
    )
    grad_video = jnp.stack([even_grad, odd_grad], 0).astype(jnp.bfloat16).reshape(video.shape)
    piece = flat_in
    both = scatter_sum(conv_part, contract_rows(piece, latent_flat))
    grad_conv, grad_down = both[:81], both[81:90]
    return (encoded_local, grad_video, grad_conv, grad_down, gain_gradient, grad_shift)


def solution(mesh):
    return jax.shard_map(
        body,
        mesh=mesh,
        in_specs=(
            P("frame", "row", None, None),
            P(),
            P(("frame", "row"), None),
            P(),
            P(),
            P(None, "row", "frame", None),
        ),
        out_specs=(
            P(None, "row", "frame", None),
            P("frame", "row", None, None),
            P(("frame", "row"), None),
            P(("frame", "row"), None),
            P(),
            P(),
        ),
        check_vma=False,
    )
```

```python
import functools
import jax
import jax.numpy as jnp
from jax import lax
from jax.experimental import pallas as pl
from jax.experimental.pallas import tpu as pltpu
from jax.sharding import PartitionSpec as P

MESH = pl.DeviceIdType.MESH
AXES = "xyz"
ORDERS = ("xyz", "yzx", "zxy")
BLOCK = 96
LANES = 128


def position():
    f, r = lax.axis_index("frame"), lax.axis_index("row")
    y = lax.div(r, 4) * 2 + lax.div(f, 8)
    pos = {"x": lax.rem(r, 4), "y": y, "z": lax.rem(lax.div(f, 2), 4)}
    return f, r, pos, lax.rem(f, 2)


def device_at(pos, core):
    frame = lax.rem(pos["y"], 2) * 8 + pos["z"] * 2 + core
    row = lax.div(pos["y"], 2) * 4 + pos["x"]
    return (frame, row)


def shifted(pos, axis, steps):
    moved = dict(pos)
    moved[axis] = lax.rem(pos[axis] + (steps + 4), 4)
    return moved


def chip_neighbours(pos, core):
    near = [device_at(shifted(pos, axis, s), core) for axis in AXES for s in (1, -1)]
    return near + [device_at(pos, 1 - core)]


def greet(devices):
    barrier = pltpu.get_barrier_semaphore()
    for device in devices:
        pl.semaphore_signal(barrier, inc=1, device_id=device, device_id_type=MESH)
    pl.semaphore_wait(barrier, len(devices))


def remote(src, dst, sems, index, device):
    return pltpu.make_async_remote_copy(
        src_ref=src,
        dst_ref=dst,
        send_sem=sems[0].at[index],
        recv_sem=sems[1].at[index],
        device_id=device,
        device_id_type=MESH,
    )


GATHER_COPIES = 16


def gather_steps(pos, core, order, buf, sems, base):
    a, b, c = order
    ca, cb, cc = pos[a], pos[b], pos[c]
    sent = []

    def start(src, dst, device):
        op = remote(src, dst, sems, base + len(sent), device)
        op.start()
        sent.append(op)
        return op

    whole = {
        c: lambda i: buf.at[core, ca, cb, i],
        b: lambda i: buf.at[core, ca, i],
        a: lambda i: buf.at[core, i],
    }
    half = BLOCK // 2
    parts = {
        c: lambda i, h: buf.at[core, ca, cb, i, pl.ds(h * half, half)],
        b: lambda i, h: buf.at[core, ca, i, pl.ds(2 * h, 2)],
        a: lambda i, h: buf.at[core, i, pl.ds(2 * h, 2)],
    }
    other = device_at(pos, 1 - core)
    for axis in (c, b, a):
        me = pos[axis]
        up, down = shifted(pos, axis, 1), shifted(pos, axis, -1)
        mine, one, ref = whole[axis](me), whole[axis], parts[axis]
        first = start(mine, mine, device_at(up, core))
        second = start(mine, mine, device_at(down, core))
        if axis == a:
            start(mine, mine, other)
        yield
        first.wait_recv()
        third = start(ref(down[axis], 0), ref(down[axis], 0), device_at(up, core))
        if axis == a:
            start(one(down[axis]), one(down[axis]), other)
        second.wait_recv()
        fourth = start(ref(up[axis], 1), ref(up[axis], 1), device_at(down, core))
        if axis == a:
            start(one(up[axis]), one(up[axis]), other)
        yield
        third.wait_recv()
        fourth.wait_recv()
    far = shifted(pos, a, 2)[a]
    start(buf.at[core, far], buf.at[core, far], other)
    yield
    for k, op in enumerate(sent):
        if k in (10, 12, 14, 15):
            op.wait_recv()
        op.wait_send()


def interleave(steps):
    steps = list(steps)
    while steps:
        left = []
        for step in steps:
            try:
                next(step)
                left.append(step)
            except StopIteration:
                pass
        steps = left


SCATTER_COPIES = 16


def add_into(count, target, terms):
    def step(i, _):
        total = terms[0](i).astype(jnp.float32)
        for term in terms[1:]:
            total = total + term(i).astype(jnp.float32)
        target(i, total)
        return 0

    lax.fori_loop(0, count, step, 0)


def scatter_steps(pos, core, order, rows, piles, got, near, q, near_q, u, near_u, sems, base, out):
    a, b, c = order
    ca, cb, cc = pos[a], pos[b], pos[c]
    half = rows // 2
    sent = []

    def start(src, dst, device):
        op = remote(src, dst, sems, base + len(sent), device)
        op.start()
        sent.append(op)
        return op

    def toward(axis, steps):
        return device_at(shifted(pos, axis, steps), core)

    def at(axis, steps):
        return shifted(pos, axis, steps)[axis]

    other = device_at(pos, 1 - core)
    far, up, down = at(a, 2), at(a, 1), at(a, -1)
    swaps = [start(piles.at[1 - core, i], got.at[i], other) for i in (far, up, down, ca)]
    yield

    def store(i):
        def put(k, total):
            piles[core, i, k] = total.astype(jnp.bfloat16)
        return put

    def pair(i, first=0):
        return [lambda k: piles[core, i, k + first], lambda k: got[i, k + first]]

    near_a, near_b, near_c, near_d = near
    swaps[0].wait_recv()
    add_into(4, store(far), pair(far))
    op_a = start(piles.at[core, far, pl.ds(0, 2)], near_a, toward(a, 1))
    op_b = start(piles.at[core, far, pl.ds(2, 2)], near_b, toward(a, -1))
    yield
    swaps[1].wait_recv()
    op_a.wait_recv()
    add_into(2, store(up), pair(up) + [lambda k: near_a[k]])
    add_into(2, lambda k, total: store(up)(k + 2, total), pair(up, 2))
    op_c = start(piles.at[core, up], near_c, toward(a, 1))
    swaps[2].wait_recv()
    op_b.wait_recv()
    add_into(2, store(down), pair(down))
    add_into(2, lambda k, total: store(down)(k + 2, total), pair(down, 2) + [lambda k: near_b[k]])
    op_d = start(piles.at[core, down], near_d, toward(a, -1))
    yield
    swaps[3].wait_recv()
    op_c.wait_recv()
    op_d.wait_recv()

    def put_q(k, total):
        q[k] = total

    add_into(4, put_q, pair(ca) + [lambda k: near_c[k], lambda k: near_d[k]])
    for axis, v, near_v, low, high, lower, upper in (
        (b, q, near_q, lambda i: q.at[i, pl.ds(0, 2)], lambda i: q.at[i, pl.ds(2, 2)],
         pl.ds(0, 2), pl.ds(2, 2)),
        (c, u, near_u, lambda i: u.at[i, pl.ds(0, half)], lambda i: u.at[i, pl.ds(half, half)],
         pl.ds(0, half), pl.ds(half, half)),
    ):
        far, up, down, me = at(axis, 2), at(axis, 1), at(axis, -1), pos[axis]
        near_a, near_b, near_c, near_d = near_v
        op_a = start(low(far), near_a, toward(axis, 1))
        op_b = start(high(far), near_b, toward(axis, -1))
        yield
        op_a.wait_recv()
        v[up, lower] = v[up, lower] + near_a[...]
        op_c = start(v.at[up], near_c, toward(axis, 1))
        op_b.wait_recv()
        v[down, upper] = v[down, upper] + near_b[...]
        op_d = start(v.at[down], near_d, toward(axis, -1))
        yield
        op_c.wait_recv()
        op_d.wait_recv()
        total = v[me] + near_c[...] + near_d[...]
        if axis == b:
            u[...] = total
        else:
            out(total)
    yield
    for op in sent:
        op.wait_send()


def scatter_scratch(rows):
    def bf(*lead):
        return pltpu.VMEM(lead + (rows, LANES), jnp.bfloat16)

    def f32(*lead):
        return pltpu.VMEM(lead + (rows, LANES), jnp.float32)

    half = pltpu.VMEM((rows // 2, LANES), jnp.float32)
    one = [bf(2, 4, 4, 4), bf(4, 4, 4), bf(2, 4), bf(2, 4), bf(4, 4), bf(4, 4), f32(4, 4),
           f32(2), f32(2), f32(4), f32(4), f32(4), half, half, f32(), f32()]
    return one


def sum_steps(f, r, x, done, row_in, frame_in, sems):
    row_in[r] = x
    ops = []
    for s in range(1, 8):
        peer = lax.rem(r + s, 8)
        op = remote(row_in.at[r], row_in.at[r], sems, s - 1, (f, peer))
        op.start()
        ops.append(op)
    yield
    for op in ops:
        op.wait_recv()
    total = row_in[0]
    for s in range(1, 8):
        total = total + row_in[s]
    frame_in[f] = total
    more = []
    for s in range(1, 16):
        peer = lax.rem(f + s, 16)
        op = remote(frame_in.at[f], frame_in.at[f], sems, 6 + s, (peer, r))
        op.start()
        more.append(op)
    yield
    for op in more:
        op.wait_recv()
    total = frame_in[0]
    for s in range(1, 16):
        total = total + frame_in[s]
    done(total)
    for op in ops + more:
        op.wait_send()


TAPS = 27
CHANS = 384
PIXELS = 256
TALLY = 16 * 16 * 128 * 12


def dot(left, right, contract=(1, 0)):
    return lax.dot_general(left, right, (((contract[0],), (contract[1],)), ((), ())),
                           preferred_element_type=jnp.float32)


def group_sum(rows, mask):
    return lax.dot_general(rows, mask, (((1,), (0,)), ((), ())),
                           precision=lax.Precision.HIGHEST, preferred_element_type=jnp.float32)


def only(condition, value):
    return jnp.where(condition, value, 0.0)


def load_rows(ref, start, count, stride):
    return jnp.concatenate([ref[j, pl.ds(start, count, stride=stride), :] for j in range(3)], 1)


def store_rows(ref, start, count, stride, value):
    for j in range(3):
        ref[j, pl.ds(start, count, stride=stride), :] = value[:, LANES * j : LANES * (j + 1)]


def halo_start(f, r, wide, lanes, out, into, sems):
    f_up, f_down = lax.rem(f + 1, 16), lax.rem(f + 15, 16)
    r_up, r_down = lax.rem(r + 1, 8), lax.rem(r + 7, 8)
    block = wide[...].reshape(16, 16, CHANS)
    store_rows(lanes, 0, PIXELS, 1, wide[...])
    ops = []

    def send(index, value, first, rows, device):
        out[first : first + rows, :] = value.astype(jnp.bfloat16)
        op = remote(out.at[pl.ds(first, rows)], into.at[pl.ds(first, rows)], sems, index, device)
        op.start()
        ops.append(op)

    send(0, block[:, 8:, :].reshape(128, CHANS), 0, 128, (f, r_up))
    send(1, block[:, :8, :].reshape(128, CHANS), 128, 128, (f, r_down))
    send(2, load_rows(lanes, 7, 32, 8), 256, 32, (f_up, r))
    send(3, load_rows(lanes, 0, 32, 8), 288, 32, (f_down, r))
    send(4, load_rows(lanes, 15, 16, 16), 320, 16, (f_up, r_up))
    send(5, load_rows(lanes, 8, 16, 16), 336, 16, (f_down, r_up))
    send(6, load_rows(lanes, 7, 16, 16), 352, 16, (f_up, r_down))
    send(7, load_rows(lanes, 0, 16, 16), 368, 16, (f_down, r_down))
    return ops


def halo_finish(f, r, ops, wide, into, ext, side, taps, first):
    for op in ops:
        op.wait_recv()
    top, bottom, left, right = r > 0, r < 7, f > 0, f < 15
    edge = into[...].astype(jnp.float32)
    middle = wide[...].reshape(16, 2, 8, CHANS)
    above = only(top, edge[0:128]).reshape(16, 1, 8, CHANS)
    below = only(bottom, edge[128:256]).reshape(16, 1, 8, CHANS)
    base = jnp.concatenate([above, middle, below], 1)
    store_rows(side, 0, 64, 1, jnp.concatenate(
        [only(left, edge[256:288]), only(right, edge[288:320])], 0))
    corner = {
        (0, 0): only(top & left, edge[320:336]),
        (0, 2): only(top & right, edge[336:352]),
        (3, 0): only(bottom & left, edge[352:368]),
        (3, 2): only(bottom & right, edge[368:384]),
    }
    for e in range(3):
        if e == 1:
            store_rows(ext, 0, 512, 1, base.reshape(512, CHANS))
        else:
            turned = pltpu.roll(base.reshape(64, 8, CHANS), 1 if e == 0 else 7, 1)
            store_rows(ext, 0, 512, 1, turned.reshape(512, CHANS))
            col = 0 if e == 0 else 7
            for i in range(4):
                if i in (0, 3):
                    value = corner[i, e]
                else:
                    value = load_rows(side, (0 if e == 0 else 32) + i - 1, 16, 2)
                store_rows(ext, 8 * i + col, 16, 32, value)
        full = load_rows(ext, 0, 512, 1).reshape(16, 32, CHANS)
        for b in range(3):
            rows = full[:, 8 * b : 8 * b + 16, :].reshape(PIXELS, CHANS)
            taps[3 * b + e, pl.ds(16 * first, PIXELS), :] = rows.astype(jnp.bfloat16)
    zeros = jnp.zeros((32, CHANS), jnp.bfloat16)
    for i in range(9):
        taps[i, pl.ds(0 if first else 256, 32), :] = zeros


def spread_start(f, r, out, into, width, sems):
    ops = []
    for s in range(1, 16):
        peer = lax.rem(f + s, 16)
        src = out.at[peer] if width == 1 else out.at[pl.ds(peer, width)]
        op = remote(src, into.at[f], sems, s - 1, (peer, r))
        op.start()
        ops.append(op)
    return ops


def pack_rows(source, first, groups, g0, size, rows, piles):
    def pack(n, _):
        g = g0 + n
        y_lo, z = lax.div(g, 4), lax.rem(g, 4)
        wide = source.at[pl.ds(pl.multiple_of(first + n * 16 * size, 8), 16 * size)]
        pad = jnp.zeros((rows - size, LANES), jnp.float32)
        for i in range(16):
            at = {"x": i % 4, "y": 2 * ((i // 4) % 2) + y_lo, "z": z}
            for j, (a, b, c) in enumerate(ORDERS):
                block = wide[size * i : size * i + size, LANES * j : LANES * (j + 1)]
                block = jnp.concatenate([block, pad], 0)
                piles[j][i // 8, at[a], at[b], at[c]] = block.astype(jnp.bfloat16)
        return 0

    lax.fori_loop(0, groups, pack, 0)


def section_kernel(video, wd, w_ref, gain_ref, shift_ref, og_ref, mask,
                   code_ref, gvideo_ref, gconv_ref, gdown_ref, ggain_ref, gshift_ref, *scratch):
    refs = list(scratch)

    def take(n):
        out = refs[:n]
        del refs[:n]
        return out

    bufs = take(3)
    big = [take(16) for _ in range(3)]
    small = [take(16) for _ in range(3)]
    (full, gbuf, wide, a_taps, g_taps, ext, side, lanes, h_out, h_in, g_out, g_in, before,
     d_out, d_in, l_out, l_in, row1, frame1, row2, frame2, act32, grad32) = take(23)
    sem = [(refs[2 * i], refs[2 * i + 1]) for i in range(len(refs) // 2)]
    s_gather, s_big, s_small, s_sum1, s_sum2, s_down, s_lat, s_act, s_grad, s_video = sem

    f, r, pos, core = position()
    peers = [(f, lax.rem(r + s, 8)) for s in range(1, 8)]
    peers += [(lax.rem(f + s, 16), r) for s in range(1, 16)]
    peers += [device_at(shifted(pos, "y", s), core) for s in (1, -1)]
    peers += [(lax.rem(f + s, 16), lax.rem(r + t, 8)) for s in (1, 15) for t in (1, 7)]
    greet(peers)
    waiting = []

    for j, (a, b, c) in enumerate(ORDERS):
        block = w_ref[:, LANES * j : LANES * (j + 1)].astype(jnp.float32)
        block = jnp.concatenate([block, jnp.zeros((BLOCK - 81, LANES), jnp.float32)], 0)
        bufs[j][core, pos[a], pos[b], pos[c]] = block.astype(jnp.bfloat16)
    weights = [gather_steps(pos, core, order, bufs[j], s_gather, j * GATHER_COPIES)
               for j, order in enumerate(ORDERS)]

    def advance(steps):
        for step in steps:
            next(step, None)

    ahead = remote(video.at[1], before, s_video, 0, (lax.rem(f + 1, 16), r))
    ahead.start()
    waiting.append(ahead)
    advance(weights)
    grad32[...] = og_ref[...].astype(jnp.float32).reshape(PIXELS, CHANS)
    grad_ops = halo_start(f, r, grad32, lanes, g_out, g_in, s_grad)
    waiting += grad_ops

    v0 = video[0].reshape(PIXELS, CHANS)
    v1 = video[1].reshape(PIXELS, CHANS)
    down = dot(v0, wd[CHANS : 2 * CHANS, :]) + dot(v1, wd[2 * CHANS :, :])
    ahead.wait_recv()
    vb = before[...].reshape(PIXELS, CHANS)
    down = down + only(f > 0, dot(vb, wd[:CHANS, :]))
    down = down.reshape(2, 16, 8, CHANS)
    d_out[...] = jnp.concatenate([down[0], down[1]], 1).astype(jnp.bfloat16)
    d_in[f] = d_out[f]
    down_ops = spread_start(f, r, d_out, d_in, 1, s_down)
    waiting += down_ops
    advance(weights)
    halo_finish(f, r, grad_ops, grad32, g_in, ext, side, g_taps, 0)
    for op in down_ops:
        op.wait_recv()
    latent = d_in[...].astype(jnp.float32).reshape(PIXELS, CHANS)

    def sum_rows(first, second):
        return jnp.concatenate([jnp.sum(first, 0, keepdims=True), jnp.sum(second, 0, keepdims=True),
                                jnp.zeros((6, CHANS), jnp.float32)], 0)

    total = []
    sums = sum_steps(f, r, sum_rows(latent, latent * latent), total.append, row1, frame1, s_sum1)
    next(sums)
    advance(weights)
    next(sums)
    advance(weights)
    next(sums, None)
    moments = group_sum(total[0], mask[...]) / TALLY
    mean = moments[0:1]
    rstd = lax.rsqrt(moments[1:2] - mean * mean + 1e-06)
    gain, shift = gain_ref[...], shift_ref[...]
    act32[...] = (latent - mean) * rstd
    xhat = act32[...]
    z = xhat * gain + shift
    grown = z / (1.0 + jnp.exp(-z))
    wide_act = gbuf.at[pl.ds(0, PIXELS)]
    wide_act[...] = grown
    act_ops = halo_start(f, r, wide_act, lanes, h_out, h_in, s_act)
    waiting += act_ops
    advance(weights)
    halo_finish(f, r, act_ops, wide_act, h_in, ext, side, a_taps, 2)

    cot = og_ref[...].reshape(PIXELS, CHANS)
    piles = [s[0] for s in big]
    for part in range(4):
        low, high = 2592 * part // CHANS, -(-2592 * (part + 1) // CHANS)

        def tap(n, _, low=low):
            k = n + low
            rows = a_taps[lax.rem(k, 9), pl.ds(pl.multiple_of(16 * lax.div(k, 9), 16), PIXELS), :]
            gbuf[pl.ds(pl.multiple_of(n * CHANS, CHANS), CHANS), :] = dot(rows, cot, (0, 0))
            return 0

        lax.fori_loop(0, high - low, tap, 0)
        pack_rows(gbuf, 2592 * part - CHANS * low, 2, 2 * part, 81, BLOCK, piles)
        if part == 1:
            advance(weights)

    def scatter(sets, rows, sems, out_ref):
        def run(j, order):
            s = sets[j]

            def out(total):
                out_ref[:, LANES * j : LANES * (j + 1)] = total[: out_ref.shape[0]]

            return scatter_steps(pos, core, order, rows, s[0], s[1], s[2:6], s[6], s[7:11],
                                 s[11], s[12:16], sems, j * SCATTER_COPIES, out)

        return [run(j, order) for j, order in enumerate(ORDERS)]

    conv_sum = scatter(big, BLOCK, s_big, gconv_ref)
    advance(conv_sum)
    for _ in range(4):
        advance(weights)

    def unpack(g, _):
        y_lo, zz = lax.div(g, 4), lax.rem(g, 4)
        for i in range(16):
            at = {"x": i % 4, "y": 2 * ((i // 4) % 2) + y_lo, "z": zz}
            for j, (a, b, c) in enumerate(ORDERS):
                block = bufs[j][i // 8, at[a], at[b], at[c]].astype(jnp.float32)
                wide[81 * i : 81 * i + 81, LANES * j : LANES * (j + 1)] = block[:81]
        full[pl.ds(pl.multiple_of(g * 1296, 16), 1296)] = wide[...].astype(jnp.bfloat16)
        return 0

    lax.fori_loop(0, 8, unpack, 0)
    advance(conv_sum)

    def back(k, acc):
        m = 26 - k
        rows = g_taps[lax.rem(m, 9), pl.ds(pl.multiple_of(16 * lax.div(m, 9), 16), PIXELS), :]
        kernel = full[pl.ds(pl.multiple_of(k * CHANS, CHANS), CHANS), :]
        return acc + dot(rows, kernel, (1, 1))

    def ahead_conv(k, acc):
        rows = a_taps[lax.rem(k, 9), pl.ds(pl.multiple_of(16 * lax.div(k, 9), 16), PIXELS), :]
        kernel = full[pl.ds(pl.multiple_of(k * CHANS, CHANS), CHANS), :]
        return acc + dot(rows, kernel)

    acc = lax.fori_loop(0, TAPS, back, jnp.zeros((PIXELS, CHANS), jnp.float32))
    xhat = act32[...]
    z = xhat * gain + shift
    sigma = 1.0 / (1.0 + jnp.exp(-z))
    pre = acc * (sigma * (1.0 + z * (1.0 - sigma)))
    wide_pre = gbuf.at[pl.ds(0, PIXELS)]
    wide_pre[...] = pre
    total2 = []
    sums2 = sum_steps(f, r, sum_rows(pre, pre * xhat), total2.append, row2, frame2, s_sum2)
    next(sums2)
    advance(conv_sum)
    next(sums2)
    acc = lax.fori_loop(0, TAPS, ahead_conv, jnp.zeros((PIXELS, CHANS), jnp.float32))
    code = acc + d_in[...].astype(jnp.float32).reshape(PIXELS, CHANS)
    code_ref[...] = code.reshape(16, 16, CHANS).astype(jnp.bfloat16)
    next(sums2, None)
    gshift_ref[...] = total2[0][0:1]
    ggain_ref[...] = total2[0][1:2]
    means = group_sum(total2[0] * gain, mask[...]) / TALLY
    grown = rstd * (wide_pre[...] * gain - means[0:1] - act32[...] * means[1:2]) + grad32[...]
    l_out[0:16] = grown.reshape(16, 16, CHANS).astype(jnp.bfloat16)
    l_out[16] = jnp.zeros((16, CHANS), jnp.bfloat16)
    l_in[f] = l_out[pl.ds(f, 2)]
    lat_ops = spread_start(f, r, l_out, l_in, 2, s_lat)
    waiting += lat_ops
    advance(conv_sum)
    for op in lat_ops:
        op.wait_recv()
    got = l_in[...].astype(jnp.float32)

    def by_rows(block):
        return jnp.concatenate([block[:, :8].reshape(128, CHANS), block[:, 8:].reshape(128, CHANS)],
                               0).astype(jnp.bfloat16)

    lat, after = by_rows(got[:, 0]), by_rows(got[:, 1])
    thin = gbuf.at[pl.ds(0, 3 * CHANS)]
    thin[0:CHANS, :] = only(f > 0, dot(before[...].reshape(PIXELS, CHANS), lat, (0, 0)))
    thin[CHANS : 2 * CHANS, :] = dot(video[0].reshape(PIXELS, CHANS), lat, (0, 0))
    thin[2 * CHANS :, :] = dot(video[1].reshape(PIXELS, CHANS), lat, (0, 0))
    pack_rows(thin, 0, 8, 0, 9, 16, [s[0] for s in small])
    down_sum = scatter(small, 16, s_small, gdown_ref)
    advance(down_sum)
    even = dot(lat, wd[CHANS : 2 * CHANS, :], (1, 1))
    odd = dot(lat, wd[2 * CHANS :, :], (1, 1)) + dot(after, wd[:CHANS, :], (1, 1))
    gvideo_ref[0] = even.reshape(2, 128, CHANS).astype(jnp.bfloat16)
    gvideo_ref[1] = odd.reshape(2, 128, CHANS).astype(jnp.bfloat16)
    interleave(conv_sum + down_sum)
    for op in waiting:
        op.wait_send()


def body(video, down_weight, conv_weight, norm_gain_vector, norm_shift_vector, output_gradient):
    lane = jnp.arange(CHANS) // 12
    mask = (lane[:, None] == lane[None, :]).astype(jnp.float32)
    vmem = pl.BlockSpec(memory_space=pltpu.VMEM)
    bf16, f32 = jnp.bfloat16, jnp.float32

    def sems(count):
        return [pltpu.SemaphoreType.DMA((count,)), pltpu.SemaphoreType.DMA((count,))]

    buf = pltpu.VMEM((2, 4, 4, 4, BLOCK, LANES), bf16)
    rows = pltpu.VMEM((384, CHANS), bf16)
    scratch = [buf] * 3 + scatter_scratch(BLOCK) * 3 + scatter_scratch(16) * 3 + [
        pltpu.VMEM((27 * CHANS, CHANS), bf16),
        pltpu.VMEM((8 * CHANS, CHANS), f32),
        pltpu.VMEM((1296, CHANS), f32),
        pltpu.VMEM((9, 288, CHANS), bf16),
        pltpu.VMEM((9, 288, CHANS), bf16),
        pltpu.VMEM((3, 512, LANES), f32),
        pltpu.VMEM((3, 64, LANES), f32),
        pltpu.VMEM((3, PIXELS, LANES), f32),
        rows, rows, rows, rows,
        pltpu.VMEM((2, 128, CHANS), bf16),
        pltpu.VMEM((16, 16, CHANS), bf16),
        pltpu.VMEM((16, 16, CHANS), bf16),
        pltpu.VMEM((17, 16, CHANS), bf16),
        pltpu.VMEM((16, 2, 16, CHANS), bf16),
        pltpu.VMEM((8, 8, CHANS), f32),
        pltpu.VMEM((16, 8, CHANS), f32),
        pltpu.VMEM((8, 8, CHANS), f32),
        pltpu.VMEM((16, 8, CHANS), f32),
        pltpu.VMEM((PIXELS, CHANS), f32),
        pltpu.VMEM((PIXELS, CHANS), f32),
    ]
    scratch += sems(48) + sems(48) + sems(48) + sems(22) + sems(22) + sems(15) + sems(15)
    scratch += sems(8) + sems(8) + sems(1)
    code, gvideo, gconv, gdown, ggain, gshift = pl.pallas_call(
        section_kernel,
        out_shape=(
            jax.ShapeDtypeStruct((16, 16, CHANS), bf16),
            jax.ShapeDtypeStruct((2, 2, 128, CHANS), bf16),
            jax.ShapeDtypeStruct((81, CHANS), f32),
            jax.ShapeDtypeStruct((9, CHANS), f32),
            jax.ShapeDtypeStruct((1, CHANS), f32),
            jax.ShapeDtypeStruct((1, CHANS), f32),
        ),
        in_specs=[vmem] * 7,
        out_specs=(vmem,) * 6,
        scratch_shapes=scratch,
        compiler_params=pltpu.CompilerParams(
            collective_id=0, has_side_effects=True, vmem_limit_bytes=63 * 2**20),
    )(video, down_weight, conv_weight, norm_gain_vector.reshape(1, CHANS),
      norm_shift_vector.reshape(1, CHANS), output_gradient.reshape(16, 16, CHANS), mask)
    return (code.reshape(16, 2, 8, CHANS), gvideo, gconv, gdown, ggain.reshape(CHANS),
            gshift.reshape(CHANS))


def solution(mesh):
    return jax.shard_map(
        body,
        mesh=mesh,
        in_specs=(
            P("frame", "row", None, None),
            P(),
            P(("frame", "row"), None),
            P(),
            P(),
            P(None, "row", "frame", None),
        ),
        out_specs=(
            P(None, "row", "frame", None),
            P("frame", "row", None, None),
            P(("frame", "row"), None),
            P(("frame", "row"), None),
            P(),
            P(),
        ),
        check_vma=False,
    )
```

```python
import functools
import jax
import jax.numpy as jnp
from jax import lax
from jax.experimental import pallas as pl
from jax.experimental.pallas import tpu as pltpu
from jax.sharding import PartitionSpec as P

MESH = pl.DeviceIdType.MESH
AXES = "xyz"
ORDERS = ("xyz", "yzx", "zxy")
BLOCK = 96
LANES = 128


def position():
    f, r = lax.axis_index("frame"), lax.axis_index("row")
    y = lax.div(r, 4) * 2 + lax.div(f, 8)
    pos = {"x": lax.rem(r, 4), "y": y, "z": lax.rem(lax.div(f, 2), 4)}
    return f, r, pos, lax.rem(f, 2)


def device_at(pos, core):
    frame = lax.rem(pos["y"], 2) * 8 + pos["z"] * 2 + core
    row = lax.div(pos["y"], 2) * 4 + pos["x"]
    return (frame, row)


def shifted(pos, axis, steps):
    moved = dict(pos)
    moved[axis] = lax.rem(pos[axis] + (steps + 4), 4)
    return moved


def chip_neighbours(pos, core):
    near = [device_at(shifted(pos, axis, s), core) for axis in AXES for s in (1, -1)]
    return near + [device_at(pos, 1 - core)]


def greet(devices):
    barrier = pltpu.get_barrier_semaphore()
    for device in devices:
        pl.semaphore_signal(barrier, inc=1, device_id=device, device_id_type=MESH)
    return lambda: pl.semaphore_wait(barrier, len(devices))


def remote(src, dst, sems, index, device):
    return pltpu.make_async_remote_copy(
        src_ref=src,
        dst_ref=dst,
        send_sem=sems[0].at[index],
        recv_sem=sems[1].at[index],
        device_id=device,
        device_id_type=MESH,
    )


GATHER_COPIES = 16


def gather_steps(pos, core, order, buf, sems, base):
    a, b, c = order
    ca, cb, cc = pos[a], pos[b], pos[c]
    sent = []

    def start(src, dst, device):
        op = remote(src, dst, sems, base + len(sent), device)
        op.start()
        sent.append(op)
        return op

    mine = buf.at[core, ca, cb, cc]
    near = [start(mine, mine, device_at(shifted(pos, c, s), core)) for s in (1, -1, 2)]
    yield
    for op in near:
        op.wait_recv()
    whole = {
        b: lambda i: buf.at[core, ca, i],
        a: lambda i: buf.at[core, i],
    }
    parts = {
        b: lambda i, h: buf.at[core, ca, i, pl.ds(2 * h, 2)],
        a: lambda i, h: buf.at[core, i, pl.ds(2 * h, 2)],
    }
    other = device_at(pos, 1 - core)
    for axis in (b, a):
        me = pos[axis]
        up, down = shifted(pos, axis, 1), shifted(pos, axis, -1)
        mine, one, ref = whole[axis](me), whole[axis], parts[axis]
        first = start(mine, mine, device_at(up, core))
        second = start(mine, mine, device_at(down, core))
        if axis == a:
            start(mine, mine, other)
        yield
        first.wait_recv()
        third = start(ref(down[axis], 0), ref(down[axis], 0), device_at(up, core))
        if axis == a:
            start(one(down[axis]), one(down[axis]), other)
        second.wait_recv()
        fourth = start(ref(up[axis], 1), ref(up[axis], 1), device_at(down, core))
        if axis == a:
            start(one(up[axis]), one(up[axis]), other)
        yield
        third.wait_recv()
        fourth.wait_recv()
    far = shifted(pos, a, 2)[a]
    start(buf.at[core, far], buf.at[core, far], other)
    yield
    for k, op in enumerate(sent):
        if k in (9, 11, 13, 14):
            op.wait_recv()
        op.wait_send()


def interleave(steps):
    steps = list(steps)
    while steps:
        left = []
        for step in steps:
            try:
                next(step)
                left.append(step)
            except StopIteration:
                pass
        steps = left


SCATTER_COPIES = 16


def add_into(count, target, terms):
    def step(i, _):
        total = terms[0](i).astype(jnp.float32)
        for term in terms[1:]:
            total = total + term(i).astype(jnp.float32)
        target(i, total)
        return 0

    lax.fori_loop(0, count, step, 0)


def scatter_steps(pos, core, order, rows, piles, got, near, q, near_q, u, near_u, sems, base, out):
    a, b, c = order
    ca, cb, cc = pos[a], pos[b], pos[c]
    sent = []

    def start(src, dst, device):
        op = remote(src, dst, sems, base + len(sent), device)
        op.start()
        sent.append(op)
        return op

    def toward(axis, steps):
        return device_at(shifted(pos, axis, steps), core)

    def at(axis, steps):
        return shifted(pos, axis, steps)[axis]

    other = device_at(pos, 1 - core)
    far, up, down = at(a, 2), at(a, 1), at(a, -1)
    swaps = [start(piles.at[1 - core, i], got.at[i], other) for i in (far, up, down, ca)]
    yield

    def store(i):
        def put(k, total):
            piles[core, i, k] = total.astype(jnp.bfloat16)
        return put

    def pair(i, first=0):
        return [lambda k: piles[core, i, k + first], lambda k: got[i, k + first]]

    near_a, near_b, near_c, near_d = near
    swaps[0].wait_recv()
    add_into(4, store(far), pair(far))
    op_a = start(piles.at[core, far, pl.ds(0, 2)], near_a, toward(a, 1))
    op_b = start(piles.at[core, far, pl.ds(2, 2)], near_b, toward(a, -1))
    yield
    swaps[1].wait_recv()
    op_a.wait_recv()
    add_into(2, store(up), pair(up) + [lambda k: near_a[k]])
    add_into(2, lambda k, total: store(up)(k + 2, total), pair(up, 2))
    op_c = start(piles.at[core, up], near_c, toward(a, 1))
    swaps[2].wait_recv()
    op_b.wait_recv()
    add_into(2, store(down), pair(down))
    add_into(2, lambda k, total: store(down)(k + 2, total), pair(down, 2) + [lambda k: near_b[k]])
    op_d = start(piles.at[core, down], near_d, toward(a, -1))
    yield
    swaps[3].wait_recv()
    op_c.wait_recv()
    op_d.wait_recv()

    def put_q(k, total):
        q[k] = total

    add_into(4, put_q, pair(ca) + [lambda k: near_c[k], lambda k: near_d[k]])
    far, up, down = at(b, 2), at(b, 1), at(b, -1)
    near_a, near_b, near_c, near_d = near_q
    op_a = start(q.at[far, pl.ds(0, 2)], near_a, toward(b, 1))
    op_b = start(q.at[far, pl.ds(2, 2)], near_b, toward(b, -1))
    yield
    op_a.wait_recv()
    q[up, pl.ds(0, 2)] = q[up, pl.ds(0, 2)] + near_a[...]
    op_c = start(q.at[up], near_c, toward(b, 1))
    op_b.wait_recv()
    q[down, pl.ds(2, 2)] = q[down, pl.ds(2, 2)] + near_b[...]
    op_d = start(q.at[down], near_d, toward(b, -1))
    yield
    op_c.wait_recv()
    op_d.wait_recv()
    u[...] = q[cb] + near_c[...] + near_d[...]
    ops = [start(u.at[at(c, s)], near_u.at[n], toward(c, s)) for n, s in enumerate((1, -1, 2))]
    yield
    for op in ops:
        op.wait_recv()
    out(u[cc] + near_u[0] + near_u[1] + near_u[2])
    yield
    for op in sent:
        op.wait_send()


def scatter_scratch(rows):
    def bf(*lead):
        return pltpu.VMEM(lead + (rows, LANES), jnp.bfloat16)

    def f32(*lead):
        return pltpu.VMEM(lead + (rows, LANES), jnp.float32)

    one = [bf(2, 4, 4, 4), bf(4, 4, 4), bf(2, 4), bf(2, 4), bf(4, 4), bf(4, 4), f32(4, 4),
           f32(2), f32(2), f32(4), f32(4), f32(4), f32(3)]
    return one


def direct_scratch(rows):
    def bf(*lead):
        return pltpu.VMEM(lead + (rows, LANES), jnp.bfloat16)

    def f32(*lead):
        return pltpu.VMEM(lead + (rows, LANES), jnp.float32)

    return [bf(2, 4, 4, 4), bf(4, 4, 4), bf(3, 4, 4), f32(4, 4), f32(3, 4), f32(4), f32(3)]


def direct_steps(pos, core, order, piles, got, near_p, q, near_q, u, near_u, sems, base, out):
    a, b, c = order
    ca = pos[a]
    sent = []

    def start(src, dst, device):
        op = remote(src, dst, sems, base + len(sent), device)
        op.start()
        sent.append(op)
        return op

    def exchange(axis, ref, near):
        return [start(ref.at[shifted(pos, axis, s)[axis]], near.at[n],
                      device_at(shifted(pos, axis, s), core)) for n, s in enumerate((1, -1, 2))]

    swap = start(piles.at[1 - core], got, device_at(pos, 1 - core))
    yield
    swap.wait_recv()
    for s in (2, 1, -1):
        i = shifted(pos, a, s)[a]
        total = piles[core, i].astype(jnp.float32) + got[i].astype(jnp.float32)
        piles[core, i] = total.astype(jnp.bfloat16)
    ops = exchange(a, piles.at[core], near_p)
    yield
    total = piles[core, ca].astype(jnp.float32) + got[ca].astype(jnp.float32)
    for n, op in enumerate(ops):
        op.wait_recv()
        total = total + near_p[n].astype(jnp.float32)
    q[...] = total
    ops = exchange(b, q, near_q)
    yield
    total = q[pos[b]]
    for n, op in enumerate(ops):
        op.wait_recv()
        total = total + near_q[n]
    u[...] = total
    ops = exchange(c, u, near_u)
    yield
    total = u[pos[c]]
    for n, op in enumerate(ops):
        op.wait_recv()
        total = total + near_u[n]
    out(total)
    yield
    for op in sent:
        op.wait_send()


def sum_steps(f, r, x, done, row_in, frame_in, sems):
    row_in[r] = x
    ops = []
    for s in range(1, 8):
        peer = lax.rem(r + s, 8)
        op = remote(row_in.at[r], row_in.at[r], sems, s - 1, (f, peer))
        op.start()
        ops.append(op)
    yield
    for op in ops:
        op.wait_recv()
    total = row_in[0]
    for s in range(1, 8):
        total = total + row_in[s]
    frame_in[f] = total
    more = []
    for s in range(1, 16):
        peer = lax.rem(f + s, 16)
        op = remote(frame_in.at[f], frame_in.at[f], sems, 6 + s, (peer, r))
        op.start()
        more.append(op)
    yield
    for op in more:
        op.wait_recv()
    total = frame_in[0]
    for s in range(1, 16):
        total = total + frame_in[s]
    done(total)
    for op in ops + more:
        op.wait_send()


TAPS = 27
CHANS = 384
PIXELS = 256
TALLY = 16 * 16 * 128 * 12


def dot(left, right, contract=(1, 0)):
    return lax.dot_general(left, right, (((contract[0],), (contract[1],)), ((), ())),
                           preferred_element_type=jnp.float32)


def group_sum(rows, mask):
    return lax.dot_general(rows, mask, (((1,), (0,)), ((), ())),
                           precision=lax.Precision.HIGHEST, preferred_element_type=jnp.float32)


def only(condition, value):
    return jnp.where(condition, value, 0.0)


def load_rows(ref, start, count, stride):
    return jnp.concatenate([ref[j, pl.ds(start, count, stride=stride), :] for j in range(3)], 1)


def store_rows(ref, start, count, stride, value):
    for j in range(3):
        ref[j, pl.ds(start, count, stride=stride), :] = value[:, LANES * j : LANES * (j + 1)]


def halo_start(f, r, wide, lanes, out, into, sems):
    f_up, f_down = lax.rem(f + 1, 16), lax.rem(f + 15, 16)
    r_up, r_down = lax.rem(r + 1, 8), lax.rem(r + 7, 8)
    block = wide[...].reshape(16, 16, CHANS)
    store_rows(lanes, 0, PIXELS, 1, wide[...])
    ops = []

    def send(index, value, first, rows, device):
        out[first : first + rows, :] = value.astype(jnp.bfloat16)
        op = remote(out.at[pl.ds(first, rows)], into.at[pl.ds(first, rows)], sems, index, device)
        op.start()
        ops.append(op)

    send(0, block[:, 8:, :].reshape(128, CHANS), 0, 128, (f, r_up))
    send(1, block[:, :8, :].reshape(128, CHANS), 128, 128, (f, r_down))
    send(2, load_rows(lanes, 7, 32, 8), 256, 32, (f_up, r))
    send(3, load_rows(lanes, 0, 32, 8), 288, 32, (f_down, r))
    send(4, load_rows(lanes, 15, 16, 16), 320, 16, (f_up, r_up))
    send(5, load_rows(lanes, 8, 16, 16), 336, 16, (f_down, r_up))
    send(6, load_rows(lanes, 7, 16, 16), 352, 16, (f_up, r_down))
    send(7, load_rows(lanes, 0, 16, 16), 368, 16, (f_down, r_down))
    return ops


def halo_finish(f, r, ops, wide, into, ext, side, taps, first):
    for op in ops:
        op.wait_recv()
    top, bottom, left, right = r > 0, r < 7, f > 0, f < 15
    edge = into[...].astype(jnp.float32)
    middle = wide[...].reshape(16, 2, 8, CHANS)
    above = only(top, edge[0:128]).reshape(16, 1, 8, CHANS)
    below = only(bottom, edge[128:256]).reshape(16, 1, 8, CHANS)
    base = jnp.concatenate([above, middle, below], 1)
    store_rows(side, 0, 64, 1, jnp.concatenate(
        [only(left, edge[256:288]), only(right, edge[288:320])], 0))
    corner = {
        (0, 0): only(top & left, edge[320:336]),
        (0, 2): only(top & right, edge[336:352]),
        (3, 0): only(bottom & left, edge[352:368]),
        (3, 2): only(bottom & right, edge[368:384]),
    }
    for e in range(3):
        if e == 1:
            store_rows(ext, 0, 512, 1, base.reshape(512, CHANS))
        else:
            turned = pltpu.roll(base.reshape(64, 8, CHANS), 1 if e == 0 else 7, 1)
            store_rows(ext, 0, 512, 1, turned.reshape(512, CHANS))
            col = 0 if e == 0 else 7
            for i in range(4):
                if i in (0, 3):
                    value = corner[i, e]
                else:
                    value = load_rows(side, (0 if e == 0 else 32) + i - 1, 16, 2)
                store_rows(ext, 8 * i + col, 16, 32, value)
        full = load_rows(ext, 0, 512, 1).reshape(16, 32, CHANS)
        for b in range(3):
            rows = full[:, 8 * b : 8 * b + 16, :].reshape(PIXELS, CHANS)
            taps[3 * b + e, pl.ds(16 * first, PIXELS), :] = rows.astype(jnp.bfloat16)
    zeros = jnp.zeros((32, CHANS), jnp.bfloat16)
    for i in range(9):
        taps[i, pl.ds(0 if first else 256, 32), :] = zeros


def spread_start(f, r, out, into, width, sems):
    ops = []
    for s in range(1, 16):
        peer = lax.rem(f + s, 16)
        src = out.at[peer] if width == 1 else out.at[pl.ds(peer, width)]
        op = remote(src, into.at[f], sems, s - 1, (peer, r))
        op.start()
        ops.append(op)
    return ops


def pack_rows(source, first, groups, g0, size, rows, piles):
    def pack(n, _):
        g = g0 + n
        y_lo, z = lax.div(g, 4), lax.rem(g, 4)
        wide = source.at[pl.ds(pl.multiple_of(first + n * 16 * size, 8), 16 * size)]
        pad = jnp.zeros((rows - size, LANES), jnp.float32)
        for i in range(16):
            at = {"x": i % 4, "y": 2 * ((i // 4) % 2) + y_lo, "z": z}
            for j, (a, b, c) in enumerate(ORDERS):
                block = wide[size * i : size * i + size, LANES * j : LANES * (j + 1)]
                block = jnp.concatenate([block, pad], 0)
                piles[j][i // 8, at[a], at[b], at[c]] = block.astype(jnp.bfloat16)
        return 0

    lax.fori_loop(0, groups, pack, 0)


def section_kernel(video, wd, w_ref, gain_ref, shift_ref, og_ref,
                   code_ref, gvideo_ref, gconv_ref, gdown_ref, ggain_ref, gshift_ref, *scratch):
    refs = list(scratch)

    def take(n):
        out = refs[:n]
        del refs[:n]
        return out

    bufs = take(3)
    big = [take(13) for _ in range(3)]
    small = [take(7) for _ in range(3)]
    (full, gbuf, wide, a_taps, g_taps, ext, side, lanes, h_out, h_in, g_out, g_in, before,
     d_out, d_in, l_out, l_in, row1, frame1, row2, frame2, act32, grad32, mask) = take(24)
    sem = [(refs[2 * i], refs[2 * i + 1]) for i in range(len(refs) // 2)]
    s_gather, s_big, s_small, s_sum1, s_sum2, s_down, s_lat, s_act, s_grad, s_video = sem

    f, r, pos, core = position()
    peers = [(f, lax.rem(r + s, 8)) for s in range(1, 8)]
    peers += [(lax.rem(f + s, 16), r) for s in range(1, 16)]
    peers += [device_at(shifted(pos, "y", s), core) for s in (1, -1)]
    peers += [(lax.rem(f + s, 16), lax.rem(r + t, 8)) for s in (1, 15) for t in (1, 7)]
    arrived = greet(peers)
    waiting = []

    def advance(steps):
        for step in steps:
            next(step, None)

    for j, (a, b, c) in enumerate(ORDERS):
        block = w_ref[:, LANES * j : LANES * (j + 1)].astype(jnp.float32)
        block = jnp.concatenate([block, jnp.zeros((BLOCK - 81, LANES), jnp.float32)], 0)
        bufs[j][core, pos[a], pos[b], pos[c]] = block.astype(jnp.bfloat16)
    grad32[...] = og_ref[...].astype(jnp.float32).reshape(PIXELS, CHANS)
    group = [jnp.floor((lax.broadcasted_iota(jnp.int32, (CHANS, CHANS), d).astype(jnp.float32) + 0.5)
                       / 12.0) for d in range(2)]
    mask[...] = jnp.where(group[0] == group[1], 1.0, 0.0)
    v0 = video[0].reshape(PIXELS, CHANS)
    v1 = video[1].reshape(PIXELS, CHANS)
    act32[...] = dot(v0, wd[CHANS : 2 * CHANS, :]) + dot(v1, wd[2 * CHANS :, :])
    arrived()

    ahead = remote(video.at[1], before, s_video, 0, (lax.rem(f + 1, 16), r))
    ahead.start()
    waiting.append(ahead)
    weights = [gather_steps(pos, core, order, bufs[j], s_gather, j * GATHER_COPIES)
               for j, order in enumerate(ORDERS)]
    advance(weights)
    grad_ops = halo_start(f, r, grad32, lanes, g_out, g_in, s_grad)
    waiting += grad_ops
    advance(weights)
    ahead.wait_recv()
    down = act32[...]
    vb = before[...].reshape(PIXELS, CHANS)
    down = down + only(f > 0, dot(vb, wd[:CHANS, :]))
    down = down.reshape(2, 16, 8, CHANS)
    d_out[...] = jnp.concatenate([down[0], down[1]], 1).astype(jnp.bfloat16)
    d_in[f] = d_out[f]
    down_ops = spread_start(f, r, d_out, d_in, 1, s_down)
    waiting += down_ops

    def sum_rows(first, second):
        return jnp.concatenate([jnp.sum(first, 0, keepdims=True), jnp.sum(second, 0, keepdims=True),
                                jnp.zeros((6, CHANS), jnp.float32)], 0)

    mine = d_out[...].astype(jnp.float32).reshape(PIXELS, CHANS)
    total = []
    sums = sum_steps(f, r, sum_rows(mine, mine * mine), total.append, row1, frame1, s_sum1)
    next(sums)
    advance(weights)
    next(sums)
    halo_finish(f, r, grad_ops, grad32, g_in, ext, side, g_taps, 0)
    advance(weights)
    for op in down_ops:
        op.wait_recv()
    latent = d_in[...].astype(jnp.float32).reshape(PIXELS, CHANS)
    next(sums, None)
    moments = group_sum(total[0], mask[...]) / TALLY
    mean = moments[0:1]
    rstd = lax.rsqrt(moments[1:2] - mean * mean + 1e-06)
    gain, shift = gain_ref[...].reshape(1, CHANS), shift_ref[...].reshape(1, CHANS)
    act32[...] = (latent - mean) * rstd
    xhat = act32[...]
    z = xhat * gain + shift
    grown = z / (1.0 + jnp.exp(-z))
    wide_act = gbuf.at[pl.ds(0, PIXELS)]
    wide_act[...] = grown
    act_ops = halo_start(f, r, wide_act, lanes, h_out, h_in, s_act)
    waiting += act_ops
    advance(weights)
    halo_finish(f, r, act_ops, wide_act, h_in, ext, side, a_taps, 2)

    cot = og_ref[...].reshape(PIXELS, CHANS)
    piles = [s[0] for s in big]
    for part in range(4):
        low, high = 2592 * part // CHANS, -(-2592 * (part + 1) // CHANS)

        def tap(n, _, low=low):
            k = n + low
            rows = a_taps[lax.rem(k, 9), pl.ds(pl.multiple_of(16 * lax.div(k, 9), 16), PIXELS), :]
            gbuf[pl.ds(pl.multiple_of(n * CHANS, CHANS), CHANS), :] = dot(rows, cot, (0, 0))
            return 0

        lax.fori_loop(0, high - low, tap, 0)
        pack_rows(gbuf, 2592 * part - CHANS * low, 2, 2 * part, 81, BLOCK, piles)

    def scatter(sets, rows, sems, out_ref):
        def run(j, order):
            s = sets[j]

            def out(total):
                out_ref[:, LANES * j : LANES * (j + 1)] = total[: out_ref.shape[0]]

            if rows == 16:
                return direct_steps(pos, core, order, *s, sems, j * SCATTER_COPIES, out)
            return scatter_steps(pos, core, order, rows, s[0], s[1], s[2:6], s[6], s[7:11],
                                 s[11], s[12], sems, j * SCATTER_COPIES, out)

        return [run(j, order) for j, order in enumerate(ORDERS)]

    conv_sum = scatter(big, BLOCK, s_big, gconv_ref)
    advance(conv_sum)
    for _ in range(3):
        advance(weights)

    def unpack(g, _):
        y_lo, zz = lax.div(g, 4), lax.rem(g, 4)
        for i in range(16):
            at = {"x": i % 4, "y": 2 * ((i // 4) % 2) + y_lo, "z": zz}
            for j, (a, b, c) in enumerate(ORDERS):
                block = bufs[j][i // 8, at[a], at[b], at[c]].astype(jnp.float32)
                wide[81 * i : 81 * i + 81, LANES * j : LANES * (j + 1)] = block[:81]
        full[pl.ds(pl.multiple_of(g * 1296, 16), 1296)] = wide[...].astype(jnp.bfloat16)
        return 0

    lax.fori_loop(0, 8, unpack, 0)
    advance(conv_sum)

    def back(n, acc):
        rows, kernels = [], []
        for e in range(3):
            k = 3 * n + e
            m = 26 - k
            rows.append(g_taps[lax.rem(m, 9), pl.ds(pl.multiple_of(16 * lax.div(m, 9), 16), PIXELS), :])
            kernels.append(full[pl.ds(pl.multiple_of(k * CHANS, CHANS), CHANS), :])
        return acc + dot(jnp.concatenate(rows, 1), jnp.concatenate(kernels, 1), (1, 1))

    def ahead_conv(n, acc):
        rows = []
        for e in range(3):
            k = 3 * n + e
            rows.append(a_taps[lax.rem(k, 9), pl.ds(pl.multiple_of(16 * lax.div(k, 9), 16), PIXELS), :])
        kernel = full[pl.ds(pl.multiple_of(n * 3 * CHANS, CHANS), 3 * CHANS), :]
        return acc + dot(jnp.concatenate(rows, 1), kernel)

    acc = jnp.zeros((PIXELS, CHANS), jnp.float32)
    acc = lax.fori_loop(0, 9, back, acc)
    xhat = act32[...]
    z = xhat * gain + shift
    sigma = 1.0 / (1.0 + jnp.exp(-z))
    pre = acc * (sigma * (1.0 + z * (1.0 - sigma)))
    wide_pre = gbuf.at[pl.ds(0, PIXELS)]
    wide_pre[...] = pre
    total2 = []
    sums2 = sum_steps(f, r, sum_rows(pre, pre * xhat), total2.append, row2, frame2, s_sum2)
    next(sums2)
    advance(conv_sum)
    acc = lax.fori_loop(0, 3, ahead_conv, jnp.zeros((PIXELS, CHANS), jnp.float32))
    next(sums2)
    acc = lax.fori_loop(3, 9, ahead_conv, acc)
    code = acc + d_in[...].astype(jnp.float32).reshape(PIXELS, CHANS)
    code_ref[...] = code.reshape(16, 16, CHANS).astype(jnp.bfloat16)
    next(sums2, None)
    gshift_ref[...] = total2[0][0:1].reshape(CHANS)
    ggain_ref[...] = total2[0][1:2].reshape(CHANS)
    means = group_sum(total2[0] * gain, mask[...]) / TALLY
    grown = rstd * (wide_pre[...] * gain - means[0:1] - act32[...] * means[1:2]) + grad32[...]
    l_out[0:16] = grown.reshape(16, 16, CHANS).astype(jnp.bfloat16)
    l_out[16] = jnp.zeros((16, CHANS), jnp.bfloat16)
    l_in[f] = l_out[pl.ds(f, 2)]
    lat_ops = spread_start(f, r, l_out, l_in, 2, s_lat)
    waiting += lat_ops
    advance(conv_sum)
    for op in lat_ops:
        op.wait_recv()
    got = l_in[...].astype(jnp.float32)

    def by_rows(block):
        return jnp.concatenate([block[:, :8].reshape(128, CHANS), block[:, 8:].reshape(128, CHANS)],
                               0).astype(jnp.bfloat16)

    lat, after = by_rows(got[:, 0]), by_rows(got[:, 1])
    thin = gbuf.at[pl.ds(0, 3 * CHANS)]
    thin[0:CHANS, :] = only(f > 0, dot(before[...].reshape(PIXELS, CHANS), lat, (0, 0)))
    thin[CHANS : 2 * CHANS, :] = dot(video[0].reshape(PIXELS, CHANS), lat, (0, 0))
    thin[2 * CHANS :, :] = dot(video[1].reshape(PIXELS, CHANS), lat, (0, 0))
    pack_rows(thin, 0, 8, 0, 9, 16, [s[0] for s in small])
    down_sum = scatter(small, 16, s_small, gdown_ref)
    advance(down_sum)
    even = dot(lat, wd[CHANS : 2 * CHANS, :], (1, 1))
    odd = dot(lat, wd[2 * CHANS :, :], (1, 1)) + dot(after, wd[:CHANS, :], (1, 1))
    gvideo_ref[0] = even.reshape(2, 128, CHANS).astype(jnp.bfloat16)
    gvideo_ref[1] = odd.reshape(2, 128, CHANS).astype(jnp.bfloat16)
    advance(down_sum)
    advance(conv_sum)
    advance(down_sum)
    advance(down_sum)
    advance(conv_sum)
    interleave(down_sum + conv_sum)
    for op in waiting:
        op.wait_send()


def hand_out(*refs):
    for source, target in zip(refs[:6], refs[6:]):
        target[...] = source[...]


def body(video, down_weight, conv_weight, norm_gain_vector, norm_shift_vector, output_gradient):
    vmem = pl.BlockSpec(memory_space=pltpu.VMEM)
    bf16, f32 = jnp.bfloat16, jnp.float32

    def sems(count):
        return [pltpu.SemaphoreType.DMA((count,)), pltpu.SemaphoreType.DMA((count,))]

    buf = pltpu.VMEM((2, 4, 4, 4, BLOCK, LANES), bf16)
    rows = pltpu.VMEM((384, CHANS), bf16)
    scratch = [buf] * 3 + scatter_scratch(BLOCK) * 3 + direct_scratch(16) * 3 + [
        pltpu.VMEM((27 * CHANS, CHANS), bf16),
        pltpu.VMEM((8 * CHANS, CHANS), f32),
        pltpu.VMEM((1296, CHANS), f32),
        pltpu.VMEM((9, 288, CHANS), bf16),
        pltpu.VMEM((9, 288, CHANS), bf16),
        pltpu.VMEM((3, 512, LANES), f32),
        pltpu.VMEM((3, 64, LANES), f32),
        pltpu.VMEM((3, PIXELS, LANES), f32),
        rows, rows, rows, rows,
        pltpu.VMEM((2, 128, CHANS), bf16),
        pltpu.VMEM((16, 16, CHANS), bf16),
        pltpu.VMEM((16, 16, CHANS), bf16),
        pltpu.VMEM((17, 16, CHANS), bf16),
        pltpu.VMEM((16, 2, 16, CHANS), bf16),
        pltpu.VMEM((8, 8, CHANS), f32),
        pltpu.VMEM((16, 8, CHANS), f32),
        pltpu.VMEM((8, 8, CHANS), f32),
        pltpu.VMEM((16, 8, CHANS), f32),
        pltpu.VMEM((PIXELS, CHANS), f32),
        pltpu.VMEM((PIXELS, CHANS), f32),
        pltpu.VMEM((CHANS, CHANS), f32),
    ]
    scratch += sems(48) + sems(48) + sems(48) + sems(22) + sems(22) + sems(15) + sems(15)
    scratch += sems(8) + sems(8) + sems(1)
    results = pl.pallas_call(
        section_kernel,
        out_shape=(
            jax.ShapeDtypeStruct((16, 16, CHANS), bf16),
            jax.ShapeDtypeStruct((2, 2, 128, CHANS), bf16),
            jax.ShapeDtypeStruct((81, CHANS), f32),
            jax.ShapeDtypeStruct((9, CHANS), f32),
            jax.ShapeDtypeStruct((CHANS,), f32),
            jax.ShapeDtypeStruct((CHANS,), f32),
        ),
        in_specs=[vmem] * 6,
        out_specs=(vmem,) * 6,
        scratch_shapes=scratch,
        compiler_params=pltpu.CompilerParams(
            collective_id=0, has_side_effects=True, vmem_limit_bytes=63 * 2**20),
    )(video, down_weight, conv_weight, norm_gain_vector, norm_shift_vector,
      output_gradient.reshape(16, 16, CHANS))
    code, gvideo, gconv, gdown, ggain, gshift = pl.pallas_call(
        hand_out,
        out_shape=tuple(jax.ShapeDtypeStruct(x.shape, x.dtype) for x in results),
        in_specs=[vmem] * 6,
        out_specs=(vmem,) * 6,
    )(*results)
    return (code.reshape(16, 2, 8, CHANS), gvideo, gconv, gdown, ggain, gshift)


def solution(mesh):
    return jax.shard_map(
        body,
        mesh=mesh,
        in_specs=(
            P("frame", "row", None, None),
            P(),
            P(("frame", "row"), None),
            P(),
            P(),
            P(None, "row", "frame", None),
        ),
        out_specs=(
            P(None, "row", "frame", None),
            P("frame", "row", None, None),
            P(("frame", "row"), None),
            P(("frame", "row"), None),
            P(),
            P(),
        ),
        check_vma=False,
    )
```

```python
import functools
import jax
import jax.numpy as jnp
from jax import lax
from jax.experimental import pallas as pl
from jax.experimental.pallas import tpu as pltpu
from jax.sharding import PartitionSpec as P

MESH = pl.DeviceIdType.MESH
AXES = "xyz"
ORDERS = ("xyz", "yzx", "zxy")
BLOCK = 96
LANES = 128


def position():
    f, r = lax.axis_index("frame"), lax.axis_index("row")
    y = lax.div(r, 4) * 2 + lax.div(f, 8)
    pos = {"x": lax.rem(r, 4), "y": y, "z": lax.rem(lax.div(f, 2), 4)}
    return f, r, pos, lax.rem(f, 2)


def device_at(pos, core):
    frame = lax.rem(pos["y"], 2) * 8 + pos["z"] * 2 + core
    row = lax.div(pos["y"], 2) * 4 + pos["x"]
    return (frame, row)


def shifted(pos, axis, steps):
    moved = dict(pos)
    moved[axis] = lax.rem(pos[axis] + (steps + 4), 4)
    return moved


def chip_neighbours(pos, core):
    near = [device_at(shifted(pos, axis, s), core) for axis in AXES for s in (1, -1)]
    return near + [device_at(pos, 1 - core)]


def greet(devices):
    barrier = pltpu.get_barrier_semaphore()
    for device in devices:
        pl.semaphore_signal(barrier, inc=1, device_id=device, device_id_type=MESH)
    return lambda: pl.semaphore_wait(barrier, len(devices))


def remote(src, dst, sems, index, device):
    return pltpu.make_async_remote_copy(
        src_ref=src,
        dst_ref=dst,
        send_sem=sems[0].at[index],
        recv_sem=sems[1].at[index],
        device_id=device,
        device_id_type=MESH,
    )


GATHER_COPIES = 20


def gather_steps(pos, core, order, buf, sems, base):
    a, b, c = order
    ca, cb, cc = pos[a], pos[b], pos[c]
    sent = []

    def start(src, dst, device):
        op = remote(src, dst, sems, base + len(sent), device)
        op.start()
        sent.append(op)
        return op

    mine = buf.at[core, ca, cb, cc]
    near = [start(mine, mine, device_at(shifted(pos, c, s), core)) for s in (1, -1, 2)]
    yield
    for op in near:
        op.wait_recv()
    whole = {
        b: lambda i: buf.at[core, ca, i],
        a: lambda i: buf.at[core, i],
    }
    parts = {
        b: lambda i, h: buf.at[core, ca, i, pl.ds(2 * h, 2)],
        a: lambda i, h: buf.at[core, i, pl.ds(2 * h, 2)],
    }
    other = device_at(pos, 1 - core)
    swaps = []
    for axis in (b, a):
        me = pos[axis]
        up, down = shifted(pos, axis, 1), shifted(pos, axis, -1)
        one, part = whole[axis], parts[axis]
        first = [start(part(me, h), part(me, h), device_at(up, core)) for h in (0,)]
        second = [start(part(me, h), part(me, h), device_at(down, core)) for h in (1,)]
        first += [start(part(me, h), part(me, h), device_at(up, core)) for h in (1,)]
        second += [start(part(me, h), part(me, h), device_at(down, core)) for h in (0,)]
        if axis == a:
            swaps.append(start(one(me), one(me), other))
        yield
        first[0].wait_recv()
        third = start(part(down[axis], 0), part(down[axis], 0), device_at(up, core))
        second[0].wait_recv()
        fourth = start(part(up[axis], 1), part(up[axis], 1), device_at(down, core))
        yield
        first[1].wait_recv()
        second[1].wait_recv()
        if axis == a:
            swaps.append(start(one(down[axis]), one(down[axis]), other))
            swaps.append(start(one(up[axis]), one(up[axis]), other))
            yield
        third.wait_recv()
        fourth.wait_recv()
    far = shifted(pos, a, 2)[a]
    swaps.append(start(buf.at[core, far], buf.at[core, far], other))
    yield
    for op in swaps:
        op.wait_recv()
    for op in sent:
        op.wait_send()


def interleave(steps):
    steps = list(steps)
    while steps:
        left = []
        for step in steps:
            try:
                next(step)
                left.append(step)
            except StopIteration:
                pass
        steps = left


SCATTER_COPIES = 20


def add_into(count, target, terms):
    def step(i, _):
        total = terms[0](i).astype(jnp.float32)
        for term in terms[1:]:
            total = total + term(i).astype(jnp.float32)
        target(i, total)
        return 0

    lax.fori_loop(0, count, step, 0)


def scatter_steps(pos, core, order, rows, piles, got, near, q, q_out, near_q, u, near_u, sems, base, out):
    a, b, c = order
    ca, cb, cc = pos[a], pos[b], pos[c]
    sent = []

    def start(src, dst, device):
        op = remote(src, dst, sems, base + len(sent), device)
        op.start()
        sent.append(op)
        return op

    def toward(axis, steps):
        return device_at(shifted(pos, axis, steps), core)

    def at(axis, steps):
        return shifted(pos, axis, steps)[axis]

    other = device_at(pos, 1 - core)
    far, up, down = at(a, 2), at(a, 1), at(a, -1)
    swaps = [start(piles.at[1 - core, i], got.at[i], other) for i in (far, up, down, ca)]
    yield

    def store(i):
        def put(k, total):
            piles[core, i, k] = total.astype(jnp.bfloat16)
        return put

    def pair(i, first=0):
        return [lambda k: piles[core, i, k + first], lambda k: got[i, k + first]]

    near_a, near_b, near_c, near_d = near
    low, high = pl.ds(0, 2), pl.ds(2, 2)
    swaps[0].wait_recv()
    add_into(4, store(far), pair(far))
    op_a = start(piles.at[core, far, low], near_a, toward(a, 1))
    op_b = start(piles.at[core, far, high], near_b, toward(a, -1))
    yield
    swaps[1].wait_recv()
    add_into(2, lambda k, total: store(up)(k + 2, total), pair(up, 2))
    late = [start(piles.at[core, up, high], near_c.at[high], toward(a, 1))]
    swaps[2].wait_recv()
    add_into(2, store(down), pair(down))
    late.append(start(piles.at[core, down, low], near_d.at[low], toward(a, -1)))
    yield
    op_a.wait_recv()
    add_into(2, store(up), pair(up) + [lambda k: near_a[k]])
    late.append(start(piles.at[core, up, low], near_c.at[low], toward(a, 1)))
    op_b.wait_recv()
    add_into(2, lambda k, total: store(down)(k + 2, total), pair(down, 2) + [lambda k: near_b[k]])
    late.append(start(piles.at[core, down, high], near_d.at[high], toward(a, -1)))
    yield
    swaps[3].wait_recv()
    for op in late:
        op.wait_recv()

    def put_q(k, total):
        q[k] = total

    add_into(4, put_q, pair(ca) + [lambda k: near_c[k], lambda k: near_d[k]])
    far, up, down = at(b, 2), at(b, 1), at(b, -1)
    near_a, near_b, near_c, near_d = near_q
    f32, bf16 = jnp.float32, jnp.bfloat16
    for s, i in ((2, far), (1, up), (3, down)):
        q_out[s] = q[i].astype(bf16)
    op_a = start(q_out.at[2, low], near_a, toward(b, 1))
    op_b = start(q_out.at[2, high], near_b, toward(b, -1))
    late = [start(q_out.at[1, high], near_c.at[high], toward(b, 1)),
            start(q_out.at[3, low], near_d.at[low], toward(b, -1))]
    yield
    op_a.wait_recv()
    q_out[1, low] = (q[up, low] + near_a[...].astype(f32)).astype(bf16)
    late.append(start(q_out.at[1, low], near_c.at[low], toward(b, 1)))
    op_b.wait_recv()
    q_out[3, high] = (q[down, high] + near_b[...].astype(f32)).astype(bf16)
    late.append(start(q_out.at[3, high], near_d.at[high], toward(b, -1)))
    yield
    for op in late:
        op.wait_recv()
    u[...] = q[cb] + near_c[...].astype(f32) + near_d[...].astype(f32)
    ops = [start(u.at[at(c, s)], near_u.at[n], toward(c, s)) for n, s in enumerate((1, -1, 2))]
    yield
    for op in ops:
        op.wait_recv()
    out(u[cc] + near_u[0] + near_u[1] + near_u[2])
    yield
    for op in sent:
        op.wait_send()


def scatter_scratch(rows):
    def bf(*lead):
        return pltpu.VMEM(lead + (rows, LANES), jnp.bfloat16)

    def f32(*lead):
        return pltpu.VMEM(lead + (rows, LANES), jnp.float32)

    one = [bf(2, 4, 4, 4), bf(4, 4, 4), bf(2, 4), bf(2, 4), bf(4, 4), bf(4, 4), f32(4, 4),
           bf(4, 4), bf(2), bf(2), bf(4), bf(4), f32(4), f32(3)]
    return one


def direct_scratch(rows):
    def bf(*lead):
        return pltpu.VMEM(lead + (rows, LANES), jnp.bfloat16)

    def f32(*lead):
        return pltpu.VMEM(lead + (rows, LANES), jnp.float32)

    return [bf(2, 4, 4, 4), bf(4, 4, 4), bf(3, 4, 4), f32(4, 4), f32(3, 4), f32(4), f32(3)]


def direct_steps(pos, core, order, piles, got, near_p, q, near_q, u, near_u, sems, base, out):
    a, b, c = order
    ca = pos[a]
    sent = []

    def start(src, dst, device):
        op = remote(src, dst, sems, base + len(sent), device)
        op.start()
        sent.append(op)
        return op

    def exchange(axis, ref, near):
        return [start(ref.at[shifted(pos, axis, s)[axis]], near.at[n],
                      device_at(shifted(pos, axis, s), core)) for n, s in enumerate((1, -1, 2))]

    swap = start(piles.at[1 - core], got, device_at(pos, 1 - core))
    yield
    swap.wait_recv()
    for s in (2, 1, -1):
        i = shifted(pos, a, s)[a]
        total = piles[core, i].astype(jnp.float32) + got[i].astype(jnp.float32)
        piles[core, i] = total.astype(jnp.bfloat16)
    ops = exchange(a, piles.at[core], near_p)
    yield
    total = piles[core, ca].astype(jnp.float32) + got[ca].astype(jnp.float32)
    for n, op in enumerate(ops):
        op.wait_recv()
        total = total + near_p[n].astype(jnp.float32)
    q[...] = total
    ops = exchange(b, q, near_q)
    yield
    total = q[pos[b]]
    for n, op in enumerate(ops):
        op.wait_recv()
        total = total + near_q[n]
    u[...] = total
    ops = exchange(c, u, near_u)
    yield
    total = u[pos[c]]
    for n, op in enumerate(ops):
        op.wait_recv()
        total = total + near_u[n]
    out(total)
    yield
    for op in sent:
        op.wait_send()


def sum_steps(f, r, x, done, row_in, frame_in, sems):
    row_in[r] = x
    ops = []
    for s in range(1, 8):
        peer = lax.rem(r + s, 8)
        op = remote(row_in.at[r], row_in.at[r], sems, s - 1, (f, peer))
        op.start()
        ops.append(op)
    yield
    for op in ops:
        op.wait_recv()
    total = row_in[0]
    for s in range(1, 8):
        total = total + row_in[s]
    frame_in[f] = total
    more = []
    for s in range(1, 16):
        peer = lax.rem(f + s, 16)
        op = remote(frame_in.at[f], frame_in.at[f], sems, 6 + s, (peer, r))
        op.start()
        more.append(op)
    yield
    for op in more:
        op.wait_recv()
    total = frame_in[0]
    for s in range(1, 16):
        total = total + frame_in[s]
    done(total)
    for op in ops + more:
        op.wait_send()


TAPS = 27
CHANS = 384
PIXELS = 256
TALLY = 16 * 16 * 128 * 12


def dot(left, right, contract=(1, 0)):
    return lax.dot_general(left, right, (((contract[0],), (contract[1],)), ((), ())),
                           preferred_element_type=jnp.float32)


def group_sum(rows, mask):
    return lax.dot_general(rows, mask, (((1,), (0,)), ((), ())),
                           precision=lax.Precision.HIGHEST, preferred_element_type=jnp.float32)


def only(condition, value):
    return jnp.where(condition, value, 0.0)


def load_rows(ref, start, count, stride):
    return jnp.concatenate([ref[j, pl.ds(start, count, stride=stride), :] for j in range(3)], 1)


def store_rows(ref, start, count, stride, value):
    for j in range(3):
        ref[j, pl.ds(start, count, stride=stride), :] = value[:, LANES * j : LANES * (j + 1)]


def halo_start(f, r, wide, lanes, out, into, sems):
    f_up, f_down = lax.rem(f + 1, 16), lax.rem(f + 15, 16)
    r_up, r_down = lax.rem(r + 1, 8), lax.rem(r + 7, 8)
    block = wide[...].reshape(16, 16, CHANS)
    store_rows(lanes, 0, PIXELS, 1, wide[...])
    ops = []

    def send(index, value, first, rows, device):
        out[first : first + rows, :] = value.astype(jnp.bfloat16)
        op = remote(out.at[pl.ds(first, rows)], into.at[pl.ds(first, rows)], sems, index, device)
        op.start()
        ops.append(op)

    send(0, block[:, 8:, :].reshape(128, CHANS), 0, 128, (f, r_up))
    send(1, block[:, :8, :].reshape(128, CHANS), 128, 128, (f, r_down))
    send(2, load_rows(lanes, 7, 32, 8), 256, 32, (f_up, r))
    send(3, load_rows(lanes, 0, 32, 8), 288, 32, (f_down, r))
    send(4, load_rows(lanes, 15, 16, 16), 320, 16, (f_up, r_up))
    send(5, load_rows(lanes, 8, 16, 16), 336, 16, (f_down, r_up))
    send(6, load_rows(lanes, 7, 16, 16), 352, 16, (f_up, r_down))
    send(7, load_rows(lanes, 0, 16, 16), 368, 16, (f_down, r_down))
    return ops


def turn(block, e):
    if e == 1:
        return block
    rows = block.reshape(-1, 8, CHANS)
    return pltpu.roll(rows, 1 if e == 0 else 7, 1).reshape(block.shape)


def put_rows(ext, e, first, value):
    for j in range(3):
        for t in range(16):
            low = 32 * t + first
            ext[3 * e + j, low : low + value.shape[1], :] = value[t, :, LANES * j : LANES * (j + 1)]


def halo_fill(wide, ext, taps, first):
    middle = wide[...].reshape(16, 2, 8, CHANS)
    for e in range(3):
        put_rows(ext, e, 8, turn(middle, e).reshape(16, 16, CHANS))
    zeros = jnp.zeros((32, CHANS), jnp.bfloat16)
    for i in range(9):
        taps[i, pl.ds(0 if first else 256, 32), :] = zeros


def halo_finish(f, r, ops, into, ext, side, taps, first):
    for op in ops:
        op.wait_recv()
    top, bottom, left, right = r > 0, r < 7, f > 0, f < 15
    edge = into[...].astype(jnp.float32)
    above = only(top, edge[0:128]).reshape(16, 8, CHANS)
    below = only(bottom, edge[128:256]).reshape(16, 8, CHANS)
    store_rows(side, 0, 64, 1, jnp.concatenate(
        [only(left, edge[256:288]), only(right, edge[288:320])], 0))
    corner = {
        (0, 0): only(top & left, edge[320:336]),
        (0, 2): only(top & right, edge[336:352]),
        (3, 0): only(bottom & left, edge[352:368]),
        (3, 2): only(bottom & right, edge[368:384]),
    }
    for e in range(3):
        put_rows(ext, e, 0, turn(above, e))
        put_rows(ext, e, 24, turn(below, e))
        shift = ext.at[pl.ds(3 * e, 3)]
        if e != 1:
            col = 0 if e == 0 else 7
            for i in range(4):
                if i in (0, 3):
                    value = corner[i, e]
                else:
                    value = load_rows(side, (0 if e == 0 else 32) + i - 1, 16, 2)
                store_rows(shift, 8 * i + col, 16, 32, value)
        full = load_rows(shift, 0, 512, 1).reshape(16, 32, CHANS)
        for b in range(3):
            block = full[:, 8 * b : 8 * b + 16, :].reshape(PIXELS, CHANS)
            taps[3 * b + e, pl.ds(16 * first, PIXELS), :] = block.astype(jnp.bfloat16)


def spread_start(f, r, out, into, width, sems):
    ops = []
    for s in range(1, 16):
        peer = lax.rem(f + s, 16)
        src = out.at[peer] if width == 1 else out.at[pl.ds(peer, width)]
        op = remote(src, into.at[f], sems, s - 1, (peer, r))
        op.start()
        ops.append(op)
    return ops


def pack_rows(source, first, groups, g0, size, rows, piles):
    def pack(n, _):
        g = g0 + n
        y_lo, z = lax.div(g, 4), lax.rem(g, 4)
        wide = source.at[pl.ds(pl.multiple_of(first + n * 16 * size, 8), 16 * size)]
        pad = jnp.zeros((rows - size, LANES), jnp.float32)
        for i in range(16):
            at = {"x": i % 4, "y": 2 * ((i // 4) % 2) + y_lo, "z": z}
            for j, (a, b, c) in enumerate(ORDERS):
                block = wide[size * i : size * i + size, LANES * j : LANES * (j + 1)]
                block = jnp.concatenate([block, pad], 0)
                piles[j][i // 8, at[a], at[b], at[c]] = block.astype(jnp.bfloat16)
        return 0

    lax.fori_loop(0, groups, pack, 0)


def section_kernel(video, wd, w_ref, gain_ref, shift_ref, og_ref,
                   code_ref, gvideo_ref, gconv_ref, gdown_ref, ggain_ref, gshift_ref, *scratch):
    refs = list(scratch)

    def take(n):
        out = refs[:n]
        del refs[:n]
        return out

    bufs = take(3)
    big = [take(14) for _ in range(3)]
    small = [take(7) for _ in range(3)]
    (full, gbuf, wide, a_taps, g_taps, ext, side, lanes, h_out, h_in, g_out, g_in, before,
     d_out, d_in, l_out, l_in, row1, frame1, row2, frame2, act32, grad32, mask) = take(24)
    sem = [(refs[2 * i], refs[2 * i + 1]) for i in range(len(refs) // 2)]
    s_gather, s_big, s_small, s_sum1, s_sum2, s_down, s_lat, s_act, s_grad, s_video = sem

    f, r, pos, core = position()
    peers = [(f, lax.rem(r + s, 8)) for s in range(1, 8)]
    peers += [(lax.rem(f + s, 16), r) for s in range(1, 16)]
    peers += [device_at(shifted(pos, "y", s), core) for s in (1, -1)]
    peers += [(lax.rem(f + s, 16), lax.rem(r + t, 8)) for s in (1, 15) for t in (1, 7)]
    arrived = greet(peers)
    waiting = []

    def advance(steps):
        for step in steps:
            next(step, None)

    for j, (a, b, c) in enumerate(ORDERS):
        block = w_ref[:, LANES * j : LANES * (j + 1)].astype(jnp.float32)
        block = jnp.concatenate([block, jnp.zeros((BLOCK - 81, LANES), jnp.float32)], 0)
        bufs[j][core, pos[a], pos[b], pos[c]] = block.astype(jnp.bfloat16)
    grad32[...] = og_ref[...].astype(jnp.float32).reshape(PIXELS, CHANS)
    group = [jnp.floor((lax.broadcasted_iota(jnp.int32, (CHANS, CHANS), d).astype(jnp.float32) + 0.5)
                       / 12.0) for d in range(2)]
    mask[...] = jnp.where(group[0] == group[1], 1.0, 0.0)
    v0 = video[0].reshape(PIXELS, CHANS)
    v1 = video[1].reshape(PIXELS, CHANS)
    act32[...] = dot(v0, wd[CHANS : 2 * CHANS, :]) + dot(v1, wd[2 * CHANS :, :])
    arrived()

    ahead = remote(video.at[1], before, s_video, 0, (lax.rem(f + 1, 16), r))
    ahead.start()
    waiting.append(ahead)
    weights = [gather_steps(pos, core, order, bufs[j], s_gather, j * GATHER_COPIES)
               for j, order in enumerate(ORDERS)]
    advance(weights)
    grad_ops = halo_start(f, r, grad32, lanes, g_out, g_in, s_grad)
    waiting += grad_ops
    advance(weights)
    halo_fill(grad32, ext, g_taps, 0)
    ahead.wait_recv()
    advance(weights)
    down = act32[...]
    vb = before[...].reshape(PIXELS, CHANS)
    down = down + only(f > 0, dot(vb, wd[:CHANS, :]))
    down = down.reshape(2, 16, 8, CHANS)
    d_out[...] = jnp.concatenate([down[0], down[1]], 1).astype(jnp.bfloat16)
    d_in[f] = d_out[f]
    down_ops = spread_start(f, r, d_out, d_in, 1, s_down)
    waiting += down_ops

    def sum_rows(first, second):
        return jnp.concatenate([jnp.sum(first, 0, keepdims=True), jnp.sum(second, 0, keepdims=True),
                                jnp.zeros((6, CHANS), jnp.float32)], 0)

    mine = d_out[...].astype(jnp.float32).reshape(PIXELS, CHANS)
    total = []
    sums = sum_steps(f, r, sum_rows(mine, mine * mine), total.append, row1, frame1, s_sum1)
    next(sums)
    next(sums)
    advance(weights)
    halo_finish(f, r, grad_ops, g_in, ext, side, g_taps, 0)
    for op in down_ops:
        op.wait_recv()
    latent = d_in[...].astype(jnp.float32).reshape(PIXELS, CHANS)
    next(sums, None)
    moments = group_sum(total[0], mask[...]) / TALLY
    mean = moments[0:1]
    rstd = lax.rsqrt(moments[1:2] - mean * mean + 1e-06)
    gain, shift = gain_ref[...].reshape(1, CHANS), shift_ref[...].reshape(1, CHANS)
    act32[...] = (latent - mean) * rstd
    xhat = act32[...]
    z = xhat * gain + shift
    grown = z / (1.0 + jnp.exp(-z))
    wide_act = gbuf.at[pl.ds(0, PIXELS)]
    wide_act[...] = grown
    act_ops = halo_start(f, r, wide_act, lanes, h_out, h_in, s_act)
    waiting += act_ops
    halo_fill(wide_act, ext, a_taps, 2)
    advance(weights)
    halo_finish(f, r, act_ops, h_in, ext, side, a_taps, 2)
    advance(weights)

    cot = og_ref[...].reshape(PIXELS, CHANS)
    piles = [s[0] for s in big]
    for part in range(4):
        low, high = 2592 * part // CHANS, -(-2592 * (part + 1) // CHANS)

        def tap(n, _, low=low):
            k = n + low
            rows = a_taps[lax.rem(k, 9), pl.ds(pl.multiple_of(16 * lax.div(k, 9), 16), PIXELS), :]
            gbuf[pl.ds(pl.multiple_of(n * CHANS, CHANS), CHANS), :] = dot(rows, cot, (0, 0))
            return 0

        lax.fori_loop(0, high - low, tap, 0)
        pack_rows(gbuf, 2592 * part - CHANS * low, 2, 2 * part, 81, BLOCK, piles)
        if part == 1:
            advance(weights)

    def scatter(sets, rows, sems, out_ref):
        def run(j, order):
            s = sets[j]

            def out(total):
                out_ref[:, LANES * j : LANES * (j + 1)] = total[: out_ref.shape[0]]

            if rows == 16:
                return direct_steps(pos, core, order, *s, sems, j * SCATTER_COPIES, out)
            return scatter_steps(pos, core, order, rows, s[0], s[1], s[2:6], s[6], s[7], s[8:12],
                                 s[12], s[13], sems, j * SCATTER_COPIES, out)

        return [run(j, order) for j, order in enumerate(ORDERS)]

    conv_sum = scatter(big, BLOCK, s_big, gconv_ref)
    advance(conv_sum)
    advance(weights)

    def unpack(g, _):
        y_lo, zz = lax.div(g, 4), lax.rem(g, 4)
        for i in range(16):
            at = {"x": i % 4, "y": 2 * ((i // 4) % 2) + y_lo, "z": zz}
            for j, (a, b, c) in enumerate(ORDERS):
                block = bufs[j][i // 8, at[a], at[b], at[c]].astype(jnp.float32)
                wide[81 * i : 81 * i + 81, LANES * j : LANES * (j + 1)] = block[:81]
        full[pl.ds(pl.multiple_of(g * 1296, 16), 1296)] = wide[...].astype(jnp.bfloat16)
        return 0

    lax.fori_loop(0, 8, unpack, 0)
    advance(conv_sum)

    def back(n, acc):
        rows, kernels = [], []
        for e in range(3):
            k = 3 * n + e
            m = 26 - k
            rows.append(g_taps[lax.rem(m, 9), pl.ds(pl.multiple_of(16 * lax.div(m, 9), 16), PIXELS), :])
            kernels.append(full[pl.ds(pl.multiple_of(k * CHANS, CHANS), CHANS), :])
        return acc + dot(jnp.concatenate(rows, 1), jnp.concatenate(kernels, 1), (1, 1))

    def ahead_conv(n, acc):
        rows = []
        for e in range(3):
            k = 3 * n + e
            rows.append(a_taps[lax.rem(k, 9), pl.ds(pl.multiple_of(16 * lax.div(k, 9), 16), PIXELS), :])
        kernel = full[pl.ds(pl.multiple_of(n * 3 * CHANS, CHANS), 3 * CHANS), :]
        return acc + dot(jnp.concatenate(rows, 1), kernel)

    acc = jnp.zeros((PIXELS, CHANS), jnp.float32)
    acc = lax.fori_loop(0, 3, back, acc)
    advance(conv_sum)
    acc = lax.fori_loop(3, 6, back, acc)
    advance(conv_sum)
    acc = lax.fori_loop(6, 9, back, acc)
    xhat = act32[...]
    z = xhat * gain + shift
    sigma = 1.0 / (1.0 + jnp.exp(-z))
    pre = acc * (sigma * (1.0 + z * (1.0 - sigma)))
    wide_pre = gbuf.at[pl.ds(0, PIXELS)]
    wide_pre[...] = pre
    total2 = []
    sums2 = sum_steps(f, r, sum_rows(pre, pre * xhat), total2.append, row2, frame2, s_sum2)
    next(sums2)
    acc = lax.fori_loop(0, 3, ahead_conv, jnp.zeros((PIXELS, CHANS), jnp.float32))
    next(sums2)
    advance(conv_sum)
    acc = lax.fori_loop(3, 5, ahead_conv, acc)
    next(sums2, None)
    gshift_ref[...] = total2[0][0:1].reshape(CHANS)
    ggain_ref[...] = total2[0][1:2].reshape(CHANS)
    means = group_sum(total2[0] * gain, mask[...]) / TALLY
    grown = rstd * (wide_pre[...] * gain - means[0:1] - act32[...] * means[1:2]) + grad32[...]
    l_out[0:16] = grown.reshape(16, 16, CHANS).astype(jnp.bfloat16)
    l_out[16] = jnp.zeros((16, CHANS), jnp.bfloat16)
    l_in[f] = l_out[pl.ds(f, 2)]
    lat_ops = spread_start(f, r, l_out, l_in, 2, s_lat)
    waiting += lat_ops
    advance(conv_sum)
    acc = lax.fori_loop(5, 9, ahead_conv, acc)
    code = acc + d_in[...].astype(jnp.float32).reshape(PIXELS, CHANS)
    code_ref[...] = code.reshape(16, 16, CHANS).astype(jnp.bfloat16)
    for op in lat_ops:
        op.wait_recv()
    got = l_in[...].astype(jnp.float32)

    def by_rows(block):
        return jnp.concatenate([block[:, :8].reshape(128, CHANS), block[:, 8:].reshape(128, CHANS)],
                               0).astype(jnp.bfloat16)

    lat, after = by_rows(got[:, 0]), by_rows(got[:, 1])
    thin = gbuf.at[pl.ds(0, 3 * CHANS)]
    thin[0:CHANS, :] = only(f > 0, dot(before[...].reshape(PIXELS, CHANS), lat, (0, 0)))
    thin[CHANS : 2 * CHANS, :] = dot(video[0].reshape(PIXELS, CHANS), lat, (0, 0))
    thin[2 * CHANS :, :] = dot(video[1].reshape(PIXELS, CHANS), lat, (0, 0))
    pack_rows(thin, 0, 8, 0, 9, 16, [s[0] for s in small])
    down_sum = scatter(small, 16, s_small, gdown_ref)
    advance(down_sum)
    advance(conv_sum)
    advance(down_sum)
    even = dot(lat, wd[CHANS : 2 * CHANS, :], (1, 1))
    odd = dot(lat, wd[2 * CHANS :, :], (1, 1)) + dot(after, wd[:CHANS, :], (1, 1))
    gvideo_ref[0] = even.reshape(2, 128, CHANS).astype(jnp.bfloat16)
    gvideo_ref[1] = odd.reshape(2, 128, CHANS).astype(jnp.bfloat16)
    advance(down_sum)
    advance(conv_sum)
    interleave(down_sum + conv_sum)
    for op in waiting:
        op.wait_send()


def hand_out(*refs):
    for source, target in zip(refs[:6], refs[6:]):
        target[...] = source[...]


def body(video, down_weight, conv_weight, norm_gain_vector, norm_shift_vector, output_gradient):
    vmem = pl.BlockSpec(memory_space=pltpu.VMEM)
    bf16, f32 = jnp.bfloat16, jnp.float32

    def sems(count):
        return [pltpu.SemaphoreType.DMA((count,)), pltpu.SemaphoreType.DMA((count,))]

    buf = pltpu.VMEM((2, 4, 4, 4, BLOCK, LANES), bf16)
    rows = pltpu.VMEM((384, CHANS), bf16)
    scratch = [buf] * 3 + scatter_scratch(BLOCK) * 3 + direct_scratch(16) * 3 + [
        pltpu.VMEM((27 * CHANS, CHANS), bf16),
        pltpu.VMEM((8 * CHANS, CHANS), f32),
        pltpu.VMEM((1296, CHANS), f32),
        pltpu.VMEM((9, 288, CHANS), bf16),
        pltpu.VMEM((9, 288, CHANS), bf16),
        pltpu.VMEM((9, 512, LANES), f32),
        pltpu.VMEM((3, 64, LANES), f32),
        pltpu.VMEM((3, PIXELS, LANES), f32),
        rows, rows, rows, rows,
        pltpu.VMEM((2, 128, CHANS), bf16),
        pltpu.VMEM((16, 16, CHANS), bf16),
        pltpu.VMEM((16, 16, CHANS), bf16),
        pltpu.VMEM((17, 16, CHANS), bf16),
        pltpu.VMEM((16, 2, 16, CHANS), bf16),
        pltpu.VMEM((8, 8, CHANS), f32),
        pltpu.VMEM((16, 8, CHANS), f32),
        pltpu.VMEM((8, 8, CHANS), f32),
        pltpu.VMEM((16, 8, CHANS), f32),
        pltpu.VMEM((PIXELS, CHANS), f32),
        pltpu.VMEM((PIXELS, CHANS), f32),
        pltpu.VMEM((CHANS, CHANS), f32),
    ]
    scratch += sems(60) + sems(60) + sems(60) + sems(22) + sems(22) + sems(15) + sems(15)
    scratch += sems(8) + sems(8) + sems(1)
    results = pl.pallas_call(
        section_kernel,
        out_shape=(
            jax.ShapeDtypeStruct((16, 16, CHANS), bf16),
            jax.ShapeDtypeStruct((2, 2, 128, CHANS), bf16),
            jax.ShapeDtypeStruct((81, CHANS), f32),
            jax.ShapeDtypeStruct((9, CHANS), f32),
            jax.ShapeDtypeStruct((CHANS,), f32),
            jax.ShapeDtypeStruct((CHANS,), f32),
        ),
        in_specs=[vmem] * 6,
        out_specs=(vmem,) * 6,
        scratch_shapes=scratch,
        compiler_params=pltpu.CompilerParams(
            collective_id=0, has_side_effects=True, vmem_limit_bytes=63 * 2**20),
    )(video, down_weight, conv_weight, norm_gain_vector, norm_shift_vector,
      output_gradient.reshape(16, 16, CHANS))
    code, gvideo, gconv, gdown, ggain, gshift = pl.pallas_call(
        hand_out,
        out_shape=tuple(jax.ShapeDtypeStruct(x.shape, x.dtype) for x in results),
        in_specs=[vmem] * 6,
        out_specs=(vmem,) * 6,
    )(*results)
    return (code.reshape(16, 2, 8, CHANS), gvideo, gconv, gdown, ggain, gshift)


def solution(mesh):
    return jax.shard_map(
        body,
        mesh=mesh,
        in_specs=(
            P("frame", "row", None, None),
            P(),
            P(("frame", "row"), None),
            P(),
            P(),
            P(None, "row", "frame", None),
        ),
        out_specs=(
            P(None, "row", "frame", None),
            P("frame", "row", None, None),
            P(("frame", "row"), None),
            P(("frame", "row"), None),
            P(),
            P(),
        ),
        check_vma=False,
    )
```

```python
import functools
import jax
import jax.numpy as jnp
from jax import lax
from jax.experimental import pallas as pl
from jax.experimental.pallas import tpu as pltpu
from jax.sharding import PartitionSpec as P

MESH = pl.DeviceIdType.MESH
AXES = "xyz"
ORDERS = ("xyz", "yzx", "zxy")
BLOCK = 96
LANES = 128


def position():
    f, r = lax.axis_index("frame"), lax.axis_index("row")
    y = lax.div(r, 4) * 2 + lax.div(f, 8)
    pos = {"x": lax.rem(r, 4), "y": y, "z": lax.rem(lax.div(f, 2), 4)}
    return f, r, pos, lax.rem(f, 2)


def device_at(pos, core):
    frame = lax.rem(pos["y"], 2) * 8 + pos["z"] * 2 + core
    row = lax.div(pos["y"], 2) * 4 + pos["x"]
    return (frame, row)


def shifted(pos, axis, steps):
    moved = dict(pos)
    moved[axis] = lax.rem(pos[axis] + (steps + 4), 4)
    return moved


def chip_neighbours(pos, core):
    near = [device_at(shifted(pos, axis, s), core) for axis in AXES for s in (1, -1)]
    return near + [device_at(pos, 1 - core)]


def greet(devices):
    barrier = pltpu.get_barrier_semaphore()
    for device in devices:
        pl.semaphore_signal(barrier, inc=1, device_id=device, device_id_type=MESH)
    return lambda: pl.semaphore_wait(barrier, len(devices))


def remote(src, dst, sems, index, device):
    return pltpu.make_async_remote_copy(
        src_ref=src,
        dst_ref=dst,
        send_sem=sems[0].at[index],
        recv_sem=sems[1].at[index],
        device_id=device,
        device_id_type=MESH,
    )


GATHER_COPIES = 20


def gather_steps(pos, core, order, buf, sems, base):
    a, b, c = order
    ca, cb, cc = pos[a], pos[b], pos[c]
    sent = []

    def start(src, dst, device):
        op = remote(src, dst, sems, base + len(sent), device)
        op.start()
        sent.append(op)
        return op

    mine = buf.at[core, ca, cb, cc]
    near = [start(mine, mine, device_at(shifted(pos, c, s), core)) for s in (1, -1, 2)]
    yield
    for op in near:
        op.wait_recv()
    whole = {
        b: lambda i: buf.at[core, ca, i],
        a: lambda i: buf.at[core, i],
    }
    parts = {
        b: lambda i, h: buf.at[core, ca, i, pl.ds(2 * h, 2)],
        a: lambda i, h: buf.at[core, i, pl.ds(2 * h, 2)],
    }
    other = device_at(pos, 1 - core)
    swaps = []
    for axis in (b, a):
        me = pos[axis]
        up, down = shifted(pos, axis, 1), shifted(pos, axis, -1)
        one, part = whole[axis], parts[axis]
        first = [start(part(me, h), part(me, h), device_at(up, core)) for h in (0,)]
        second = [start(part(me, h), part(me, h), device_at(down, core)) for h in (1,)]
        first += [start(part(me, h), part(me, h), device_at(up, core)) for h in (1,)]
        second += [start(part(me, h), part(me, h), device_at(down, core)) for h in (0,)]
        if axis == a:
            swaps.append(start(one(me), one(me), other))
        yield
        first[0].wait_recv()
        third = start(part(down[axis], 0), part(down[axis], 0), device_at(up, core))
        second[0].wait_recv()
        fourth = start(part(up[axis], 1), part(up[axis], 1), device_at(down, core))
        yield
        first[1].wait_recv()
        second[1].wait_recv()
        if axis == a:
            swaps.append(start(one(down[axis]), one(down[axis]), other))
            swaps.append(start(one(up[axis]), one(up[axis]), other))
            yield
        third.wait_recv()
        fourth.wait_recv()
    far = shifted(pos, a, 2)[a]
    swaps.append(start(buf.at[core, far], buf.at[core, far], other))
    yield
    for op in swaps:
        op.wait_recv()
    for op in sent:
        op.wait_send()


def interleave(steps):
    steps = list(steps)
    while steps:
        left = []
        for step in steps:
            try:
                next(step)
                left.append(step)
            except StopIteration:
                pass
        steps = left


SCATTER_COPIES = 20


def add_into(count, target, terms):
    def step(i, _):
        total = terms[0](i).astype(jnp.float32)
        for term in terms[1:]:
            total = total + term(i).astype(jnp.float32)
        target(i, total)
        return 0

    lax.fori_loop(0, count, step, 0)


def scatter_steps(pos, core, order, rows, piles, got, near, q, q_out, near_q, u, near_u, sems, base, out):
    a, b, c = order
    ca, cb, cc = pos[a], pos[b], pos[c]
    sent = []

    def start(src, dst, device):
        op = remote(src, dst, sems, base + len(sent), device)
        op.start()
        sent.append(op)
        return op

    def toward(axis, steps):
        return device_at(shifted(pos, axis, steps), core)

    def at(axis, steps):
        return shifted(pos, axis, steps)[axis]

    other = device_at(pos, 1 - core)
    far, up, down = at(a, 2), at(a, 1), at(a, -1)
    swaps = [start(piles.at[1 - core, i], got.at[i], other) for i in (far, up, down, ca)]
    yield

    def store(i):
        def put(k, total):
            piles[core, i, k] = total.astype(jnp.bfloat16)
        return put

    def pair(i, first=0):
        return [lambda k: piles[core, i, k + first], lambda k: got[i, k + first]]

    near_a, near_b, near_c, near_d = near
    low, high = pl.ds(0, 2), pl.ds(2, 2)
    swaps[0].wait_recv()
    add_into(4, store(far), pair(far))
    op_a = start(piles.at[core, far, low], near_a, toward(a, 1))
    op_b = start(piles.at[core, far, high], near_b, toward(a, -1))
    yield
    swaps[1].wait_recv()
    add_into(2, lambda k, total: store(up)(k + 2, total), pair(up, 2))
    late = [start(piles.at[core, up, high], near_c.at[high], toward(a, 1))]
    swaps[2].wait_recv()
    add_into(2, store(down), pair(down))
    late.append(start(piles.at[core, down, low], near_d.at[low], toward(a, -1)))
    yield
    op_a.wait_recv()
    add_into(2, store(up), pair(up) + [lambda k: near_a[k]])
    late.append(start(piles.at[core, up, low], near_c.at[low], toward(a, 1)))
    op_b.wait_recv()
    add_into(2, lambda k, total: store(down)(k + 2, total), pair(down, 2) + [lambda k: near_b[k]])
    late.append(start(piles.at[core, down, high], near_d.at[high], toward(a, -1)))
    yield
    swaps[3].wait_recv()
    for op in late:
        op.wait_recv()

    def put_q(k, total):
        q[k] = total

    add_into(4, put_q, pair(ca) + [lambda k: near_c[k], lambda k: near_d[k]])
    far, up, down = at(b, 2), at(b, 1), at(b, -1)
    near_a, near_b, near_c, near_d = near_q
    f32, bf16 = jnp.float32, jnp.bfloat16
    for s, i in ((2, far), (1, up), (3, down)):
        q_out[s] = q[i].astype(bf16)
    op_a = start(q_out.at[2, low], near_a, toward(b, 1))
    op_b = start(q_out.at[2, high], near_b, toward(b, -1))
    late = [start(q_out.at[1, high], near_c.at[high], toward(b, 1)),
            start(q_out.at[3, low], near_d.at[low], toward(b, -1))]
    yield
    op_a.wait_recv()
    q_out[1, low] = (q[up, low] + near_a[...].astype(f32)).astype(bf16)
    late.append(start(q_out.at[1, low], near_c.at[low], toward(b, 1)))
    op_b.wait_recv()
    q_out[3, high] = (q[down, high] + near_b[...].astype(f32)).astype(bf16)
    late.append(start(q_out.at[3, high], near_d.at[high], toward(b, -1)))
    yield
    for op in late:
        op.wait_recv()
    u[...] = q[cb] + near_c[...].astype(f32) + near_d[...].astype(f32)
    ops = [start(u.at[at(c, s)], near_u.at[n], toward(c, s)) for n, s in enumerate((1, -1, 2))]
    yield
    for op in ops:
        op.wait_recv()
    out(u[cc] + near_u[0] + near_u[1] + near_u[2])
    yield
    for op in sent:
        op.wait_send()


def scatter_scratch(rows):
    def bf(*lead):
        return pltpu.VMEM(lead + (rows, LANES), jnp.bfloat16)

    def f32(*lead):
        return pltpu.VMEM(lead + (rows, LANES), jnp.float32)

    one = [bf(2, 4, 4, 4), bf(4, 4, 4), bf(2, 4), bf(2, 4), bf(4, 4), bf(4, 4), f32(4, 4),
           bf(4, 4), bf(2), bf(2), bf(4), bf(4), f32(4), f32(3)]
    return one


def direct_scratch(rows):
    def bf(*lead):
        return pltpu.VMEM(lead + (rows, LANES), jnp.bfloat16)

    def f32(*lead):
        return pltpu.VMEM(lead + (rows, LANES), jnp.float32)

    return [bf(2, 4, 4, 4), bf(4, 4, 4), bf(3, 4, 4), f32(4, 4), bf(4, 4), bf(3, 4), f32(4), f32(3)]


def direct_steps(pos, core, order, piles, got, near_p, q, q_out, near_q, u, near_u, sems, base, out):
    a, b, c = order
    ca = pos[a]
    sent = []

    def start(src, dst, device):
        op = remote(src, dst, sems, base + len(sent), device)
        op.start()
        sent.append(op)
        return op

    def exchange(axis, ref, near):
        return [start(ref.at[shifted(pos, axis, s)[axis]], near.at[n],
                      device_at(shifted(pos, axis, s), core)) for n, s in enumerate((1, -1, 2))]

    swap = start(piles.at[1 - core], got, device_at(pos, 1 - core))
    yield
    swap.wait_recv()
    for s in (2, 1, -1):
        i = shifted(pos, a, s)[a]
        total = piles[core, i].astype(jnp.float32) + got[i].astype(jnp.float32)
        piles[core, i] = total.astype(jnp.bfloat16)
    ops = exchange(a, piles.at[core], near_p)
    yield
    total = piles[core, ca].astype(jnp.float32) + got[ca].astype(jnp.float32)
    for n, op in enumerate(ops):
        op.wait_recv()
        total = total + near_p[n].astype(jnp.float32)
    q[...] = total
    q_out[...] = total.astype(jnp.bfloat16)
    ops = exchange(b, q_out, near_q)
    yield
    total = q[pos[b]]
    for n, op in enumerate(ops):
        op.wait_recv()
        total = total + near_q[n].astype(jnp.float32)
    u[...] = total
    ops = exchange(c, u, near_u)
    yield
    total = u[pos[c]]
    for n, op in enumerate(ops):
        op.wait_recv()
        total = total + near_u[n]
    out(total)
    yield
    for op in sent:
        op.wait_send()


def sum_steps(f, r, x, done, row_in, frame_in, sems):
    row_in[r] = x
    ops = []
    for s in range(1, 8):
        peer = lax.rem(r + s, 8)
        op = remote(row_in.at[r], row_in.at[r], sems, s - 1, (f, peer))
        op.start()
        ops.append(op)
    yield
    for op in ops:
        op.wait_recv()
    total = row_in[0]
    for s in range(1, 8):
        total = total + row_in[s]
    frame_in[f] = total
    more = []
    for s in range(1, 16):
        peer = lax.rem(f + s, 16)
        op = remote(frame_in.at[f], frame_in.at[f], sems, 6 + s, (peer, r))
        op.start()
        more.append(op)
    yield
    for op in more:
        op.wait_recv()
    total = frame_in[0]
    for s in range(1, 16):
        total = total + frame_in[s]
    done(total)
    for op in ops + more:
        op.wait_send()


TAPS = 27
CHANS = 384
PIXELS = 256
TALLY = 16 * 16 * 128 * 12


def dot(left, right, contract=(1, 0)):
    return lax.dot_general(left, right, (((contract[0],), (contract[1],)), ((), ())),
                           preferred_element_type=jnp.float32)


def group_sum(rows, mask):
    return lax.dot_general(rows, mask, (((1,), (0,)), ((), ())),
                           precision=lax.Precision.HIGHEST, preferred_element_type=jnp.float32)


def only(condition, value):
    return jnp.where(condition, value, 0.0)


def load_rows(ref, start, count, stride):
    return jnp.concatenate([ref[j, pl.ds(start, count, stride=stride), :] for j in range(3)], 1)


def store_rows(ref, start, count, stride, value):
    for j in range(3):
        ref[j, pl.ds(start, count, stride=stride), :] = value[:, LANES * j : LANES * (j + 1)]


def halo_start(f, r, wide, lanes, out, into, sems):
    f_up, f_down = lax.rem(f + 1, 16), lax.rem(f + 15, 16)
    r_up, r_down = lax.rem(r + 1, 8), lax.rem(r + 7, 8)
    block = wide[...].reshape(16, 16, CHANS)
    store_rows(lanes, 0, PIXELS, 1, wide[...])
    ops = []

    def send(index, value, first, rows, device):
        out[first : first + rows, :] = value.astype(jnp.bfloat16)
        op = remote(out.at[pl.ds(first, rows)], into.at[pl.ds(first, rows)], sems, index, device)
        op.start()
        ops.append(op)

    send(0, block[:, 8:, :].reshape(128, CHANS), 0, 128, (f, r_up))
    send(1, block[:, :8, :].reshape(128, CHANS), 128, 128, (f, r_down))
    send(2, load_rows(lanes, 7, 32, 8), 256, 32, (f_up, r))
    send(3, load_rows(lanes, 0, 32, 8), 288, 32, (f_down, r))
    send(4, load_rows(lanes, 15, 16, 16), 320, 16, (f_up, r_up))
    send(5, load_rows(lanes, 8, 16, 16), 336, 16, (f_down, r_up))
    send(6, load_rows(lanes, 7, 16, 16), 352, 16, (f_up, r_down))
    send(7, load_rows(lanes, 0, 16, 16), 368, 16, (f_down, r_down))
    return ops


def turn(block, e):
    if e == 1:
        return block
    rows = block.reshape(-1, 8, CHANS)
    return pltpu.roll(rows, 1 if e == 0 else 7, 1).reshape(block.shape)


def put_rows(ext, e, first, value):
    for j in range(3):
        for t in range(16):
            low = 32 * t + first
            ext[3 * e + j, low : low + value.shape[1], :] = value[t, :, LANES * j : LANES * (j + 1)]


def halo_fill(wide, ext, taps, first):
    middle = wide[...].reshape(16, 2, 8, CHANS)
    for e in range(3):
        put_rows(ext, e, 8, turn(middle, e).reshape(16, 16, CHANS))
    zeros = jnp.zeros((32, CHANS), jnp.bfloat16)
    for i in range(9):
        taps[i, pl.ds(0 if first else 256, 32), :] = zeros


def halo_finish(f, r, ops, into, ext, side, taps, first):
    for op in ops:
        op.wait_recv()
    top, bottom, left, right = r > 0, r < 7, f > 0, f < 15
    edge = into[...].astype(jnp.float32)
    above = only(top, edge[0:128]).reshape(16, 8, CHANS)
    below = only(bottom, edge[128:256]).reshape(16, 8, CHANS)
    store_rows(side, 0, 64, 1, jnp.concatenate(
        [only(left, edge[256:288]), only(right, edge[288:320])], 0))
    corner = {
        (0, 0): only(top & left, edge[320:336]),
        (0, 2): only(top & right, edge[336:352]),
        (3, 0): only(bottom & left, edge[352:368]),
        (3, 2): only(bottom & right, edge[368:384]),
    }
    for e in range(3):
        put_rows(ext, e, 0, turn(above, e))
        put_rows(ext, e, 24, turn(below, e))
        shift = ext.at[pl.ds(3 * e, 3)]
        if e != 1:
            col = 0 if e == 0 else 7
            for i in range(4):
                if i in (0, 3):
                    value = corner[i, e]
                else:
                    value = load_rows(side, (0 if e == 0 else 32) + i - 1, 16, 2)
                store_rows(shift, 8 * i + col, 16, 32, value)
        full = load_rows(shift, 0, 512, 1).reshape(16, 32, CHANS)
        for b in range(3):
            block = full[:, 8 * b : 8 * b + 16, :].reshape(PIXELS, CHANS)
            taps[3 * b + e, pl.ds(16 * first, PIXELS), :] = block.astype(jnp.bfloat16)


def spread_start(f, r, out, into, width, sems):
    ops = []
    for s in range(1, 16):
        peer = lax.rem(f + s, 16)
        src = out.at[peer] if width == 1 else out.at[pl.ds(peer, width)]
        op = remote(src, into.at[f], sems, s - 1, (peer, r))
        op.start()
        ops.append(op)
    return ops


def pack_rows(source, first, groups, g0, size, rows, piles):
    def pack(n, _):
        g = g0 + n
        y_lo, z = lax.div(g, 4), lax.rem(g, 4)
        wide = source.at[pl.ds(pl.multiple_of(first + n * 16 * size, 8), 16 * size)]
        pad = jnp.zeros((rows - size, LANES), jnp.float32)
        for i in range(16):
            at = {"x": i % 4, "y": 2 * ((i // 4) % 2) + y_lo, "z": z}
            for j, (a, b, c) in enumerate(ORDERS):
                block = wide[size * i : size * i + size, LANES * j : LANES * (j + 1)]
                block = jnp.concatenate([block, pad], 0)
                piles[j][i // 8, at[a], at[b], at[c]] = block.astype(jnp.bfloat16)
        return 0

    lax.fori_loop(0, groups, pack, 0)


def section_kernel(video_any, wd_any, w_any, gain_ref, shift_ref, og_any,
                   code_ref, gvideo_ref, gconv_ref, gdown_ref, ggain_ref, gshift_ref, *scratch):
    refs = list(scratch)

    def take(n):
        out = refs[:n]
        del refs[:n]
        return out

    bufs = take(3)
    big = [take(14) for _ in range(3)]
    small = [take(8) for _ in range(3)]
    (full, gbuf, wide, a_taps, g_taps, ext, side, lanes, h_out, h_in, g_out, g_in, before,
     d_out, d_in, l_out, l_in, row1, frame1, row2, frame2, act32, grad32, mask, video, wd, w_ref, og_ref, s_local) = take(29)
    sem = [(refs[2 * i], refs[2 * i + 1]) for i in range(len(refs) // 2)]
    s_gather, s_big, s_small, s_sum1, s_sum2, s_down, s_lat, s_act, s_grad, s_video = sem

    f, r, pos, core = position()
    peers = [(f, lax.rem(r + s, 8)) for s in range(1, 8)]
    peers += [(lax.rem(f + s, 16), r) for s in range(1, 16)]
    peers += [device_at(shifted(pos, "y", s), core) for s in (1, -1)]
    peers += [(lax.rem(f + s, 16), lax.rem(r + t, 8)) for s in (1, 15) for t in (1, 7)]
    arrived = greet(peers)
    fetch = [pltpu.make_async_copy(src, dst, s_local.at[n]) for n, (src, dst) in enumerate(
        ((w_any, w_ref), (og_any, og_ref), (video_any, video), (wd_any, wd)))]
    for op in fetch:
        op.start()
    waiting = []

    def advance(steps):
        for step in steps:
            next(step, None)

    fetch[0].wait()
    for j, (a, b, c) in enumerate(ORDERS):
        block = w_ref[:, LANES * j : LANES * (j + 1)].astype(jnp.float32)
        block = jnp.concatenate([block, jnp.zeros((BLOCK - 81, LANES), jnp.float32)], 0)
        bufs[j][core, pos[a], pos[b], pos[c]] = block.astype(jnp.bfloat16)
    fetch[1].wait()
    grad32[...] = og_ref[...].astype(jnp.float32).reshape(PIXELS, CHANS)
    group = [jnp.floor((lax.broadcasted_iota(jnp.int32, (CHANS, CHANS), d).astype(jnp.float32) + 0.5)
                       / 12.0) for d in range(2)]
    mask[...] = jnp.where(group[0] == group[1], 1.0, 0.0)
    fetch[2].wait()
    fetch[3].wait()
    v0 = video[0].reshape(PIXELS, CHANS)
    v1 = video[1].reshape(PIXELS, CHANS)
    act32[...] = dot(v0, wd[CHANS : 2 * CHANS, :]) + dot(v1, wd[2 * CHANS :, :])
    arrived()

    ahead = remote(video.at[1], before, s_video, 0, (lax.rem(f + 1, 16), r))
    ahead.start()
    waiting.append(ahead)
    weights = [gather_steps(pos, core, order, bufs[j], s_gather, j * GATHER_COPIES)
               for j, order in enumerate(ORDERS)]
    advance(weights)
    grad_ops = halo_start(f, r, grad32, lanes, g_out, g_in, s_grad)
    waiting += grad_ops
    advance(weights)
    halo_fill(grad32, ext, g_taps, 0)
    ahead.wait_recv()
    advance(weights)
    down = act32[...]
    vb = before[...].reshape(PIXELS, CHANS)
    down = down + only(f > 0, dot(vb, wd[:CHANS, :]))
    down = down.reshape(2, 16, 8, CHANS)
    d_out[...] = jnp.concatenate([down[0], down[1]], 1).astype(jnp.bfloat16)
    d_in[f] = d_out[f]
    down_ops = spread_start(f, r, d_out, d_in, 1, s_down)
    waiting += down_ops

    def sum_rows(first, second):
        return jnp.concatenate([jnp.sum(first, 0, keepdims=True), jnp.sum(second, 0, keepdims=True),
                                jnp.zeros((6, CHANS), jnp.float32)], 0)

    mine = d_out[...].astype(jnp.float32).reshape(PIXELS, CHANS)
    total = []
    sums = sum_steps(f, r, sum_rows(mine, mine * mine), total.append, row1, frame1, s_sum1)
    next(sums)
    next(sums)
    advance(weights)
    halo_finish(f, r, grad_ops, g_in, ext, side, g_taps, 0)
    for op in down_ops:
        op.wait_recv()
    latent = d_in[...].astype(jnp.float32).reshape(PIXELS, CHANS)
    next(sums, None)
    moments = group_sum(total[0], mask[...]) / TALLY
    mean = moments[0:1]
    rstd = lax.rsqrt(moments[1:2] - mean * mean + 1e-06)
    gain, shift = gain_ref[...].reshape(1, CHANS), shift_ref[...].reshape(1, CHANS)
    act32[...] = (latent - mean) * rstd
    xhat = act32[...]
    z = xhat * gain + shift
    grown = z / (1.0 + jnp.exp(-z))
    wide_act = gbuf.at[pl.ds(0, PIXELS)]
    wide_act[...] = grown
    act_ops = halo_start(f, r, wide_act, lanes, h_out, h_in, s_act)
    waiting += act_ops
    halo_fill(wide_act, ext, a_taps, 2)
    advance(weights)
    halo_finish(f, r, act_ops, h_in, ext, side, a_taps, 2)
    advance(weights)

    cot = og_ref[...].reshape(PIXELS, CHANS)
    piles = [s[0] for s in big]
    for part in range(4):
        low, high = 2592 * part // CHANS, -(-2592 * (part + 1) // CHANS)

        def tap(n, _, low=low):
            k = n + low
            rows = a_taps[lax.rem(k, 9), pl.ds(pl.multiple_of(16 * lax.div(k, 9), 16), PIXELS), :]
            gbuf[pl.ds(pl.multiple_of(n * CHANS, CHANS), CHANS), :] = dot(rows, cot, (0, 0))
            return 0

        lax.fori_loop(0, high - low, tap, 0)
        pack_rows(gbuf, 2592 * part - CHANS * low, 2, 2 * part, 81, BLOCK, piles)
        if part == 1:
            advance(weights)

    def scatter(sets, rows, sems, out_ref):
        def run(j, order):
            s = sets[j]

            def out(total):
                out_ref[:, LANES * j : LANES * (j + 1)] = total[: out_ref.shape[0]]

            if rows == 16:
                return direct_steps(pos, core, order, *s, sems, j * SCATTER_COPIES, out)
            return scatter_steps(pos, core, order, rows, s[0], s[1], s[2:6], s[6], s[7], s[8:12],
                                 s[12], s[13], sems, j * SCATTER_COPIES, out)

        return [run(j, order) for j, order in enumerate(ORDERS)]

    conv_sum = scatter(big, BLOCK, s_big, gconv_ref)
    advance(conv_sum)
    advance(weights)

    def unpack(g, _):
        y_lo, zz = lax.div(g, 4), lax.rem(g, 4)
        for i in range(16):
            at = {"x": i % 4, "y": 2 * ((i // 4) % 2) + y_lo, "z": zz}
            for j, (a, b, c) in enumerate(ORDERS):
                block = bufs[j][i // 8, at[a], at[b], at[c]].astype(jnp.float32)
                wide[81 * i : 81 * i + 81, LANES * j : LANES * (j + 1)] = block[:81]
        full[pl.ds(pl.multiple_of(g * 1296, 16), 1296)] = wide[...].astype(jnp.bfloat16)
        return 0

    lax.fori_loop(0, 8, unpack, 0)
    advance(conv_sum)

    def back(n, acc):
        rows, kernels = [], []
        for e in range(3):
            k = 3 * n + e
            m = 26 - k
            rows.append(g_taps[lax.rem(m, 9), pl.ds(pl.multiple_of(16 * lax.div(m, 9), 16), PIXELS), :])
            kernels.append(full[pl.ds(pl.multiple_of(k * CHANS, CHANS), CHANS), :])
        return acc + dot(jnp.concatenate(rows, 1), jnp.concatenate(kernels, 1), (1, 1))

    def ahead_conv(n, acc):
        rows = []
        for e in range(3):
            k = 3 * n + e
            rows.append(a_taps[lax.rem(k, 9), pl.ds(pl.multiple_of(16 * lax.div(k, 9), 16), PIXELS), :])
        kernel = full[pl.ds(pl.multiple_of(n * 3 * CHANS, CHANS), 3 * CHANS), :]
        return acc + dot(jnp.concatenate(rows, 1), kernel)

    acc = jnp.zeros((PIXELS, CHANS), jnp.float32)
    acc = lax.fori_loop(0, 3, back, acc)
    advance(conv_sum)
    acc = lax.fori_loop(3, 6, back, acc)
    advance(conv_sum)
    acc = lax.fori_loop(6, 9, back, acc)
    xhat = act32[...]
    z = xhat * gain + shift
    sigma = 1.0 / (1.0 + jnp.exp(-z))
    pre = acc * (sigma * (1.0 + z * (1.0 - sigma)))
    wide_pre = gbuf.at[pl.ds(0, PIXELS)]
    wide_pre[...] = pre
    total2 = []
    sums2 = sum_steps(f, r, sum_rows(pre, pre * xhat), total2.append, row2, frame2, s_sum2)
    next(sums2)
    acc = lax.fori_loop(0, 3, ahead_conv, jnp.zeros((PIXELS, CHANS), jnp.float32))
    next(sums2)
    advance(conv_sum)
    acc = lax.fori_loop(3, 5, ahead_conv, acc)
    next(sums2, None)
    gshift_ref[...] = total2[0][0:1].reshape(CHANS)
    ggain_ref[...] = total2[0][1:2].reshape(CHANS)
    means = group_sum(total2[0] * gain, mask[...]) / TALLY
    grown = rstd * (wide_pre[...] * gain - means[0:1] - act32[...] * means[1:2]) + grad32[...]
    l_out[0:16] = grown.reshape(16, 16, CHANS).astype(jnp.bfloat16)
    l_out[16] = jnp.zeros((16, CHANS), jnp.bfloat16)
    l_in[f] = l_out[pl.ds(f, 2)]
    lat_ops = spread_start(f, r, l_out, l_in, 2, s_lat)
    waiting += lat_ops
    advance(conv_sum)
    acc = lax.fori_loop(5, 9, ahead_conv, acc)
    code = acc + d_in[...].astype(jnp.float32).reshape(PIXELS, CHANS)
    code_ref[...] = code.reshape(16, 16, CHANS).astype(jnp.bfloat16)
    for op in lat_ops:
        op.wait_recv()
    got = l_in[...].astype(jnp.float32)

    def by_rows(block):
        return jnp.concatenate([block[:, :8].reshape(128, CHANS), block[:, 8:].reshape(128, CHANS)],
                               0).astype(jnp.bfloat16)

    lat, after = by_rows(got[:, 0]), by_rows(got[:, 1])
    thin = gbuf.at[pl.ds(0, 3 * CHANS)]
    thin[0:CHANS, :] = only(f > 0, dot(before[...].reshape(PIXELS, CHANS), lat, (0, 0)))
    thin[CHANS : 2 * CHANS, :] = dot(video[0].reshape(PIXELS, CHANS), lat, (0, 0))
    thin[2 * CHANS :, :] = dot(video[1].reshape(PIXELS, CHANS), lat, (0, 0))
    pack_rows(thin, 0, 8, 0, 9, 16, [s[0] for s in small])
    down_sum = scatter(small, 16, s_small, gdown_ref)
    advance(down_sum)
    advance(conv_sum)
    advance(down_sum)
    even = dot(lat, wd[CHANS : 2 * CHANS, :], (1, 1))
    odd = dot(lat, wd[2 * CHANS :, :], (1, 1)) + dot(after, wd[:CHANS, :], (1, 1))
    gvideo_ref[0] = even.reshape(2, 128, CHANS).astype(jnp.bfloat16)
    gvideo_ref[1] = odd.reshape(2, 128, CHANS).astype(jnp.bfloat16)
    advance(down_sum)
    advance(conv_sum)
    interleave(down_sum + conv_sum)
    for op in waiting:
        op.wait_send()


def hand_out(*refs):
    for source, target in zip(refs[:6], refs[6:]):
        target[...] = source[...]


def body(video, down_weight, conv_weight, norm_gain_vector, norm_shift_vector, output_gradient):
    vmem = pl.BlockSpec(memory_space=pltpu.VMEM)
    anywhere = pl.BlockSpec(memory_space=pl.ANY)
    bf16, f32 = jnp.bfloat16, jnp.float32

    def sems(count):
        return [pltpu.SemaphoreType.DMA((count,)), pltpu.SemaphoreType.DMA((count,))]

    buf = pltpu.VMEM((2, 4, 4, 4, BLOCK, LANES), bf16)
    rows = pltpu.VMEM((384, CHANS), bf16)
    scratch = [buf] * 3 + scatter_scratch(BLOCK) * 3 + direct_scratch(16) * 3 + [
        pltpu.VMEM((27 * CHANS, CHANS), bf16),
        pltpu.VMEM((8 * CHANS, CHANS), f32),
        pltpu.VMEM((1296, CHANS), f32),
        pltpu.VMEM((9, 288, CHANS), bf16),
        pltpu.VMEM((9, 288, CHANS), bf16),
        pltpu.VMEM((9, 512, LANES), f32),
        pltpu.VMEM((3, 64, LANES), f32),
        pltpu.VMEM((3, PIXELS, LANES), f32),
        rows, rows, rows, rows,
        pltpu.VMEM((2, 128, CHANS), bf16),
        pltpu.VMEM((16, 16, CHANS), bf16),
        pltpu.VMEM((16, 16, CHANS), bf16),
        pltpu.VMEM((17, 16, CHANS), bf16),
        pltpu.VMEM((16, 2, 16, CHANS), bf16),
        pltpu.VMEM((8, 8, CHANS), f32),
        pltpu.VMEM((16, 8, CHANS), f32),
        pltpu.VMEM((8, 8, CHANS), f32),
        pltpu.VMEM((16, 8, CHANS), f32),
        pltpu.VMEM((PIXELS, CHANS), f32),
        pltpu.VMEM((PIXELS, CHANS), f32),
        pltpu.VMEM((CHANS, CHANS), f32),
        pltpu.VMEM((2, 2, 128, CHANS), bf16),
        pltpu.VMEM((3 * CHANS, CHANS), bf16),
        pltpu.VMEM((81, CHANS), bf16),
        pltpu.VMEM((16, 16, CHANS), bf16),
        pltpu.SemaphoreType.DMA((4,)),
    ]
    scratch += sems(60) + sems(60) + sems(60) + sems(22) + sems(22) + sems(15) + sems(15)
    scratch += sems(8) + sems(8) + sems(1)
    results = pl.pallas_call(
        section_kernel,
        out_shape=(
            jax.ShapeDtypeStruct((16, 16, CHANS), bf16),
            jax.ShapeDtypeStruct((2, 2, 128, CHANS), bf16),
            jax.ShapeDtypeStruct((81, CHANS), f32),
            jax.ShapeDtypeStruct((9, CHANS), f32),
            jax.ShapeDtypeStruct((CHANS,), f32),
            jax.ShapeDtypeStruct((CHANS,), f32),
        ),
        in_specs=[anywhere] * 3 + [vmem] * 2 + [anywhere],
        out_specs=(vmem,) * 6,
        scratch_shapes=scratch,
        compiler_params=pltpu.CompilerParams(
            collective_id=0, has_side_effects=True, vmem_limit_bytes=63 * 2**20),
    )(video, down_weight, conv_weight, norm_gain_vector, norm_shift_vector,
      output_gradient.reshape(16, 16, CHANS))
    code, gvideo, gconv, gdown, ggain, gshift = pl.pallas_call(
        hand_out,
        out_shape=tuple(jax.ShapeDtypeStruct(x.shape, x.dtype) for x in results),
        in_specs=[vmem] * 6,
        out_specs=(vmem,) * 6,
    )(*results)
    return (code.reshape(16, 2, 8, CHANS), gvideo, gconv, gdown, ggain, gshift)


def solution(mesh):
    return jax.shard_map(
        body,
        mesh=mesh,
        in_specs=(
            P("frame", "row", None, None),
            P(),
            P(("frame", "row"), None),
            P(),
            P(),
            P(None, "row", "frame", None),
        ),
        out_specs=(
            P(None, "row", "frame", None),
            P("frame", "row", None, None),
            P(("frame", "row"), None),
            P(("frame", "row"), None),
            P(),
            P(),
        ),
        check_vma=False,
    )
```

```python
import functools
import jax
import jax.numpy as jnp
from jax import lax
from jax.experimental import pallas as pl
from jax.experimental.pallas import tpu as pltpu
from jax.sharding import PartitionSpec as P

MESH = pl.DeviceIdType.MESH
AXES = "xyz"
ORDERS = ("xyz", "yzx", "zxy")
BLOCK = 96
LANES = 128


def position():
    f, r = lax.axis_index("frame"), lax.axis_index("row")
    y = lax.div(r, 4) * 2 + lax.div(f, 8)
    pos = {"x": lax.rem(r, 4), "y": y, "z": lax.rem(lax.div(f, 2), 4)}
    return f, r, pos, lax.rem(f, 2)


def device_at(pos, core):
    frame = lax.rem(pos["y"], 2) * 8 + pos["z"] * 2 + core
    row = lax.div(pos["y"], 2) * 4 + pos["x"]
    return (frame, row)


def shifted(pos, axis, steps):
    moved = dict(pos)
    moved[axis] = lax.rem(pos[axis] + (steps + 4), 4)
    return moved


def chip_neighbours(pos, core):
    near = [device_at(shifted(pos, axis, s), core) for axis in AXES for s in (1, -1)]
    return near + [device_at(pos, 1 - core)]


def greet(devices):
    barrier = pltpu.get_barrier_semaphore()
    for device in devices:
        pl.semaphore_signal(barrier, inc=1, device_id=device, device_id_type=MESH)
    return lambda: pl.semaphore_wait(barrier, len(devices))


def remote(src, dst, sems, index, device):
    return pltpu.make_async_remote_copy(
        src_ref=src,
        dst_ref=dst,
        send_sem=sems[0].at[index],
        recv_sem=sems[1].at[index],
        device_id=device,
        device_id_type=MESH,
    )


GATHER_COPIES = 20


def gather_steps(pos, core, order, buf, sems, base):
    a, b, c = order
    ca, cb, cc = pos[a], pos[b], pos[c]
    sent = []

    def start(src, dst, device):
        op = remote(src, dst, sems, base + len(sent), device)
        op.start()
        sent.append(op)
        return op

    mine = buf.at[core, ca, cb, cc]
    near = [start(mine, mine, device_at(shifted(pos, c, s), core)) for s in (1, -1, 2)]
    yield
    for op in near:
        op.wait_recv()
    whole = {
        b: lambda i: buf.at[core, ca, i],
        a: lambda i: buf.at[core, i],
    }
    parts = {
        b: lambda i, h: buf.at[core, ca, i, pl.ds(2 * h, 2)],
        a: lambda i, h: buf.at[core, i, pl.ds(2 * h, 2)],
    }
    other = device_at(pos, 1 - core)
    swaps = []
    for axis in (b, a):
        me = pos[axis]
        up, down = shifted(pos, axis, 1), shifted(pos, axis, -1)
        one, part = whole[axis], parts[axis]
        first = [start(part(me, h), part(me, h), device_at(up, core)) for h in (0,)]
        second = [start(part(me, h), part(me, h), device_at(down, core)) for h in (1,)]
        first += [start(part(me, h), part(me, h), device_at(up, core)) for h in (1,)]
        second += [start(part(me, h), part(me, h), device_at(down, core)) for h in (0,)]
        if axis == a:
            swaps.append(start(one(me), one(me), other))
        yield
        first[0].wait_recv()
        third = start(part(down[axis], 0), part(down[axis], 0), device_at(up, core))
        second[0].wait_recv()
        fourth = start(part(up[axis], 1), part(up[axis], 1), device_at(down, core))
        yield
        first[1].wait_recv()
        second[1].wait_recv()
        if axis == a:
            swaps.append(start(one(down[axis]), one(down[axis]), other))
            swaps.append(start(one(up[axis]), one(up[axis]), other))
            yield
        third.wait_recv()
        fourth.wait_recv()
    far = shifted(pos, a, 2)[a]
    swaps.append(start(buf.at[core, far], buf.at[core, far], other))
    yield
    for op in swaps:
        op.wait_recv()
    for op in sent:
        op.wait_send()


def interleave(steps):
    steps = list(steps)
    while steps:
        left = []
        for step in steps:
            try:
                next(step)
                left.append(step)
            except StopIteration:
                pass
        steps = left


SCATTER_COPIES = 20


def add_into(count, target, terms):
    def step(i, _):
        total = terms[0](i).astype(jnp.float32)
        for term in terms[1:]:
            total = total + term(i).astype(jnp.float32)
        target(i, total)
        return 0

    lax.fori_loop(0, count, step, 0)


def scatter_steps(pos, core, order, rows, piles, got, near, q, q_out, near_q, u, near_u, sems, base, out):
    a, b, c = order
    ca, cb, cc = pos[a], pos[b], pos[c]
    sent = []

    def start(src, dst, device):
        op = remote(src, dst, sems, base + len(sent), device)
        op.start()
        sent.append(op)
        return op

    def toward(axis, steps):
        return device_at(shifted(pos, axis, steps), core)

    def at(axis, steps):
        return shifted(pos, axis, steps)[axis]

    other = device_at(pos, 1 - core)
    far, up, down = at(a, 2), at(a, 1), at(a, -1)
    swaps = [start(piles.at[1 - core, i], got.at[i], other) for i in (far, up, down, ca)]
    yield

    def store(i):
        def put(k, total):
            piles[core, i, k] = total.astype(jnp.bfloat16)
        return put

    def pair(i, first=0):
        return [lambda k: piles[core, i, k + first], lambda k: got[i, k + first]]

    near_a, near_b, near_c, near_d = near
    low, high = pl.ds(0, 2), pl.ds(2, 2)
    swaps[0].wait_recv()
    add_into(4, store(far), pair(far))
    op_a = start(piles.at[core, far, low], near_a, toward(a, 1))
    op_b = start(piles.at[core, far, high], near_b, toward(a, -1))
    yield
    swaps[1].wait_recv()
    add_into(2, lambda k, total: store(up)(k + 2, total), pair(up, 2))
    late = [start(piles.at[core, up, high], near_c.at[high], toward(a, 1))]
    swaps[2].wait_recv()
    add_into(2, store(down), pair(down))
    late.append(start(piles.at[core, down, low], near_d.at[low], toward(a, -1)))
    yield
    op_a.wait_recv()
    add_into(2, store(up), pair(up) + [lambda k: near_a[k]])
    late.append(start(piles.at[core, up, low], near_c.at[low], toward(a, 1)))
    op_b.wait_recv()
    add_into(2, lambda k, total: store(down)(k + 2, total), pair(down, 2) + [lambda k: near_b[k]])
    late.append(start(piles.at[core, down, high], near_d.at[high], toward(a, -1)))
    yield
    swaps[3].wait_recv()
    for op in late:
        op.wait_recv()

    def put_q(k, total):
        q[k] = total

    add_into(4, put_q, pair(ca) + [lambda k: near_c[k], lambda k: near_d[k]])
    far, up, down = at(b, 2), at(b, 1), at(b, -1)
    near_a, near_b, near_c, near_d = near_q
    f32, bf16 = jnp.float32, jnp.bfloat16
    for s, i in ((2, far), (1, up), (3, down)):
        q_out[s] = q[i].astype(bf16)
    op_a = start(q_out.at[2, low], near_a, toward(b, 1))
    op_b = start(q_out.at[2, high], near_b, toward(b, -1))
    late = [start(q_out.at[1, high], near_c.at[high], toward(b, 1)),
            start(q_out.at[3, low], near_d.at[low], toward(b, -1))]
    yield
    op_a.wait_recv()
    q_out[1, low] = (q[up, low] + near_a[...].astype(f32)).astype(bf16)
    late.append(start(q_out.at[1, low], near_c.at[low], toward(b, 1)))
    op_b.wait_recv()
    q_out[3, high] = (q[down, high] + near_b[...].astype(f32)).astype(bf16)
    late.append(start(q_out.at[3, high], near_d.at[high], toward(b, -1)))
    yield
    for op in late:
        op.wait_recv()
    u[...] = q[cb] + near_c[...].astype(f32) + near_d[...].astype(f32)
    ops = [start(u.at[at(c, s)], near_u.at[n], toward(c, s)) for n, s in enumerate((1, -1, 2))]
    yield
    for op in ops:
        op.wait_recv()
    out(u[cc] + near_u[0] + near_u[1] + near_u[2])
    yield
    for op in sent:
        op.wait_send()


def scatter_scratch(rows):
    def bf(*lead):
        return pltpu.VMEM(lead + (rows, LANES), jnp.bfloat16)

    def f32(*lead):
        return pltpu.VMEM(lead + (rows, LANES), jnp.float32)

    one = [bf(2, 4, 4, 4), bf(4, 4, 4), bf(2, 4), bf(2, 4), bf(4, 4), bf(4, 4), f32(4, 4),
           bf(4, 4), bf(2), bf(2), bf(4), bf(4), f32(4), f32(3)]
    return one


def direct_scratch(rows):
    def bf(*lead):
        return pltpu.VMEM(lead + (rows, LANES), jnp.bfloat16)

    def f32(*lead):
        return pltpu.VMEM(lead + (rows, LANES), jnp.float32)

    return [bf(2, 4, 4, 4), bf(4, 4, 4), bf(3, 4, 4), f32(4, 4), bf(4, 4), bf(3, 4), f32(4), f32(3)]


def direct_steps(pos, core, order, piles, got, near_p, q, q_out, near_q, u, near_u, sems, base, out):
    a, b, c = order
    ca = pos[a]
    sent = []

    def start(src, dst, device):
        op = remote(src, dst, sems, base + len(sent), device)
        op.start()
        sent.append(op)
        return op

    def exchange(axis, ref, near):
        return [start(ref.at[shifted(pos, axis, s)[axis]], near.at[n],
                      device_at(shifted(pos, axis, s), core)) for n, s in enumerate((1, -1, 2))]

    places = [shifted(pos, a, s)[a] for s in (2, 1, -1, 0)]
    swaps = [start(piles.at[1 - core, i], got.at[i], device_at(pos, 1 - core)) for i in places]
    yield
    ops = []
    for n, s in enumerate((2, 1, -1)):
        i = places[n]
        swaps[n].wait_recv()
        total = piles[core, i].astype(jnp.float32) + got[i].astype(jnp.float32)
        piles[core, i] = total.astype(jnp.bfloat16)
        ops.append(start(piles.at[core, i], near_p.at[n], device_at(shifted(pos, a, s), core)))
    yield
    swaps[3].wait_recv()
    total = piles[core, ca].astype(jnp.float32) + got[ca].astype(jnp.float32)
    for n, op in enumerate(ops):
        op.wait_recv()
        total = total + near_p[n].astype(jnp.float32)
    q[...] = total
    q_out[...] = total.astype(jnp.bfloat16)
    ops = exchange(b, q_out, near_q)
    yield
    total = q[pos[b]]
    for n, op in enumerate(ops):
        op.wait_recv()
        total = total + near_q[n].astype(jnp.float32)
    u[...] = total
    ops = exchange(c, u, near_u)
    yield
    total = u[pos[c]]
    for n, op in enumerate(ops):
        op.wait_recv()
        total = total + near_u[n]
    out(total)
    yield
    for op in sent:
        op.wait_send()


def sum_steps(f, r, x, done, row_in, frame_in, sems):
    row_in[r] = x
    ops = []
    for s in range(1, 8):
        peer = lax.rem(r + s, 8)
        op = remote(row_in.at[r], row_in.at[r], sems, s - 1, (f, peer))
        op.start()
        ops.append(op)
    yield
    for op in ops:
        op.wait_recv()
    total = row_in[0]
    for s in range(1, 8):
        total = total + row_in[s]
    frame_in[f] = total
    more = []
    for s in range(1, 16):
        peer = lax.rem(f + s, 16)
        op = remote(frame_in.at[f], frame_in.at[f], sems, 6 + s, (peer, r))
        op.start()
        more.append(op)
    yield
    for op in more:
        op.wait_recv()
    total = frame_in[0]
    for s in range(1, 16):
        total = total + frame_in[s]
    done(total)
    for op in ops + more:
        op.wait_send()


TAPS = 27
CHANS = 384
PIXELS = 256
TALLY = 16 * 16 * 128 * 12


def dot(left, right, contract=(1, 0)):
    return lax.dot_general(left, right, (((contract[0],), (contract[1],)), ((), ())),
                           preferred_element_type=jnp.float32)


def group_sum(rows, mask):
    return lax.dot_general(rows, mask, (((1,), (0,)), ((), ())),
                           precision=lax.Precision.HIGHEST, preferred_element_type=jnp.float32)


def only(condition, value):
    return jnp.where(condition, value, 0.0)


def load_rows(ref, start, count, stride):
    return jnp.concatenate([ref[j, pl.ds(start, count, stride=stride), :] for j in range(3)], 1)


def store_rows(ref, start, count, stride, value):
    for j in range(3):
        ref[j, pl.ds(start, count, stride=stride), :] = value[:, LANES * j : LANES * (j + 1)]


def halo_start(f, r, wide, lanes, out, into, sems):
    f_up, f_down = lax.rem(f + 1, 16), lax.rem(f + 15, 16)
    r_up, r_down = lax.rem(r + 1, 8), lax.rem(r + 7, 8)
    block = wide[...].reshape(16, 16, CHANS)
    store_rows(lanes, 0, PIXELS, 1, wide[...])
    ops = []

    def send(index, value, first, rows, device):
        out[first : first + rows, :] = value.astype(jnp.bfloat16)
        op = remote(out.at[pl.ds(first, rows)], into.at[pl.ds(first, rows)], sems, index, device)
        op.start()
        ops.append(op)

    send(0, block[:, 8:, :].reshape(128, CHANS), 0, 128, (f, r_up))
    send(1, block[:, :8, :].reshape(128, CHANS), 128, 128, (f, r_down))
    send(2, load_rows(lanes, 7, 32, 8), 256, 32, (f_up, r))
    send(3, load_rows(lanes, 0, 32, 8), 288, 32, (f_down, r))
    send(4, load_rows(lanes, 15, 16, 16), 320, 16, (f_up, r_up))
    send(5, load_rows(lanes, 8, 16, 16), 336, 16, (f_down, r_up))
    send(6, load_rows(lanes, 7, 16, 16), 352, 16, (f_up, r_down))
    send(7, load_rows(lanes, 0, 16, 16), 368, 16, (f_down, r_down))
    return ops


def turn(block, e):
    if e == 1:
        return block
    rows = block.reshape(-1, 8, CHANS)
    return pltpu.roll(rows, 1 if e == 0 else 7, 1).reshape(block.shape)


def put_rows(ext, e, first, value):
    for j in range(3):
        for t in range(16):
            low = 32 * t + first
            ext[3 * e + j, low : low + value.shape[1], :] = value[t, :, LANES * j : LANES * (j + 1)]


def halo_fill(wide, ext, taps, first):
    middle = wide[...].reshape(16, 2, 8, CHANS)
    for e in range(3):
        put_rows(ext, e, 8, turn(middle, e).reshape(16, 16, CHANS))
    zeros = jnp.zeros((32, CHANS), jnp.bfloat16)
    for i in range(9):
        taps[i, pl.ds(0 if first else 256, 32), :] = zeros


def halo_finish(f, r, ops, into, ext, side, taps, first):
    for op in ops:
        op.wait_recv()
    top, bottom, left, right = r > 0, r < 7, f > 0, f < 15
    edge = into[...].astype(jnp.float32)
    above = only(top, edge[0:128]).reshape(16, 8, CHANS)
    below = only(bottom, edge[128:256]).reshape(16, 8, CHANS)
    store_rows(side, 0, 64, 1, jnp.concatenate(
        [only(left, edge[256:288]), only(right, edge[288:320])], 0))
    corner = {
        (0, 0): only(top & left, edge[320:336]),
        (0, 2): only(top & right, edge[336:352]),
        (3, 0): only(bottom & left, edge[352:368]),
        (3, 2): only(bottom & right, edge[368:384]),
    }
    for e in range(3):
        put_rows(ext, e, 0, turn(above, e))
        put_rows(ext, e, 24, turn(below, e))
        shift = ext.at[pl.ds(3 * e, 3)]
        if e != 1:
            col = 0 if e == 0 else 7
            for i in range(4):
                if i in (0, 3):
                    value = corner[i, e]
                else:
                    value = load_rows(side, (0 if e == 0 else 32) + i - 1, 16, 2)
                store_rows(shift, 8 * i + col, 16, 32, value)
        full = load_rows(shift, 0, 512, 1).reshape(16, 32, CHANS)
        for b in range(3):
            block = full[:, 8 * b : 8 * b + 16, :].reshape(PIXELS, CHANS)
            taps[3 * b + e, pl.ds(16 * first, PIXELS), :] = block.astype(jnp.bfloat16)


def spread_start(f, r, out, into, width, sems):
    ops = []
    for s in range(1, 16):
        peer = lax.rem(f + s, 16)
        src = out.at[peer] if width == 1 else out.at[pl.ds(peer, width)]
        op = remote(src, into.at[f], sems, s - 1, (peer, r))
        op.start()
        ops.append(op)
    return ops


def pack_rows(source, first, groups, g0, size, rows, piles):
    def pack(n, _):
        g = g0 + n
        y_lo, z = lax.div(g, 4), lax.rem(g, 4)
        wide = source.at[pl.ds(pl.multiple_of(first + n * 16 * size, 8), 16 * size)]
        pad = jnp.zeros((rows - size, LANES), jnp.float32)
        for i in range(16):
            at = {"x": i % 4, "y": 2 * ((i // 4) % 2) + y_lo, "z": z}
            for j, (a, b, c) in enumerate(ORDERS):
                block = wide[size * i : size * i + size, LANES * j : LANES * (j + 1)]
                block = jnp.concatenate([block, pad], 0)
                piles[j][i // 8, at[a], at[b], at[c]] = block.astype(jnp.bfloat16)
        return 0

    lax.fori_loop(0, groups, pack, 0)


def section_kernel(video_any, wd_any, w_any, gain_ref, shift_ref, og_any,
                   code_ref, gvideo_ref, gconv_ref, gdown_ref, ggain_ref, gshift_ref, *scratch):
    refs = list(scratch)

    def take(n):
        out = refs[:n]
        del refs[:n]
        return out

    bufs = take(3)
    big = [take(14) for _ in range(3)]
    small = [take(8) for _ in range(3)]
    (full, gbuf, wide, a_taps, g_taps, ext, side, lanes, h_out, h_in, g_out, g_in, before,
     d_out, d_in, l_out, l_in, row1, frame1, row2, frame2, act32, grad32, mask, video, wd, w_ref, og_ref, s_local) = take(29)
    sem = [(refs[2 * i], refs[2 * i + 1]) for i in range(len(refs) // 2)]
    s_gather, s_big, s_small, s_sum1, s_sum2, s_down, s_lat, s_act, s_grad, s_video = sem

    f, r, pos, core = position()
    peers = [(f, lax.rem(r + s, 8)) for s in range(1, 8)]
    peers += [(lax.rem(f + s, 16), r) for s in range(1, 16)]
    peers += [device_at(shifted(pos, "y", s), core) for s in (1, -1)]
    peers += [(lax.rem(f + s, 16), lax.rem(r + t, 8)) for s in (1, 15) for t in (1, 7)]
    arrived = greet(peers)
    fetch = [pltpu.make_async_copy(src, dst, s_local.at[n]) for n, (src, dst) in enumerate(
        ((w_any, w_ref), (og_any, og_ref), (video_any, video), (wd_any, wd)))]
    for op in fetch:
        op.start()
    waiting = []

    def advance(steps):
        for step in steps:
            next(step, None)

    fetch[0].wait()
    for j, (a, b, c) in enumerate(ORDERS):
        block = w_ref[:, LANES * j : LANES * (j + 1)].astype(jnp.float32)
        block = jnp.concatenate([block, jnp.zeros((BLOCK - 81, LANES), jnp.float32)], 0)
        bufs[j][core, pos[a], pos[b], pos[c]] = block.astype(jnp.bfloat16)
    fetch[1].wait()
    grad32[...] = og_ref[...].astype(jnp.float32).reshape(PIXELS, CHANS)
    group = [jnp.floor((lax.broadcasted_iota(jnp.int32, (CHANS, CHANS), d).astype(jnp.float32) + 0.5)
                       / 12.0) for d in range(2)]
    mask[...] = jnp.where(group[0] == group[1], 1.0, 0.0)
    fetch[2].wait()
    fetch[3].wait()
    v0 = video[0].reshape(PIXELS, CHANS)
    v1 = video[1].reshape(PIXELS, CHANS)
    act32[...] = dot(v0, wd[CHANS : 2 * CHANS, :]) + dot(v1, wd[2 * CHANS :, :])
    arrived()

    ahead = remote(video.at[1], before, s_video, 0, (lax.rem(f + 1, 16), r))
    ahead.start()
    waiting.append(ahead)
    weights = [gather_steps(pos, core, order, bufs[j], s_gather, j * GATHER_COPIES)
               for j, order in enumerate(ORDERS)]
    advance(weights)
    grad_ops = halo_start(f, r, grad32, lanes, g_out, g_in, s_grad)
    waiting += grad_ops
    advance(weights)
    halo_fill(grad32, ext, g_taps, 0)
    ahead.wait_recv()
    advance(weights)
    down = act32[...]
    vb = before[...].reshape(PIXELS, CHANS)
    down = down + only(f > 0, dot(vb, wd[:CHANS, :]))
    down = down.reshape(2, 16, 8, CHANS)
    d_out[...] = jnp.concatenate([down[0], down[1]], 1).astype(jnp.bfloat16)
    d_in[f] = d_out[f]
    down_ops = spread_start(f, r, d_out, d_in, 1, s_down)
    waiting += down_ops

    def sum_rows(first, second):
        return jnp.concatenate([jnp.sum(first, 0, keepdims=True), jnp.sum(second, 0, keepdims=True),
                                jnp.zeros((6, CHANS), jnp.float32)], 0)

    mine = d_out[...].astype(jnp.float32).reshape(PIXELS, CHANS)
    total = []
    sums = sum_steps(f, r, sum_rows(mine, mine * mine), total.append, row1, frame1, s_sum1)
    next(sums)
    next(sums)
    advance(weights)
    halo_finish(f, r, grad_ops, g_in, ext, side, g_taps, 0)
    for op in down_ops:
        op.wait_recv()
    latent = d_in[...].astype(jnp.float32).reshape(PIXELS, CHANS)
    next(sums, None)
    moments = group_sum(total[0], mask[...]) / TALLY
    mean = moments[0:1]
    rstd = lax.rsqrt(moments[1:2] - mean * mean + 1e-06)
    gain, shift = gain_ref[...].reshape(1, CHANS), shift_ref[...].reshape(1, CHANS)
    act32[...] = (latent - mean) * rstd
    xhat = act32[...]
    z = xhat * gain + shift
    grown = z / (1.0 + jnp.exp(-z))
    wide_act = gbuf.at[pl.ds(0, PIXELS)]
    wide_act[...] = grown
    act_ops = halo_start(f, r, wide_act, lanes, h_out, h_in, s_act)
    waiting += act_ops
    halo_fill(wide_act, ext, a_taps, 2)
    advance(weights)
    halo_finish(f, r, act_ops, h_in, ext, side, a_taps, 2)
    advance(weights)

    cot = og_ref[...].reshape(PIXELS, CHANS)
    piles = [s[0] for s in big]
    for part in range(4):
        low, high = 2592 * part // CHANS, -(-2592 * (part + 1) // CHANS)

        def tap(n, _, low=low):
            k = n + low
            rows = a_taps[lax.rem(k, 9), pl.ds(pl.multiple_of(16 * lax.div(k, 9), 16), PIXELS), :]
            gbuf[pl.ds(pl.multiple_of(n * CHANS, CHANS), CHANS), :] = dot(rows, cot, (0, 0))
            return 0

        lax.fori_loop(0, high - low, tap, 0)
        pack_rows(gbuf, 2592 * part - CHANS * low, 2, 2 * part, 81, BLOCK, piles)
        if part == 1:
            advance(weights)

    def scatter(sets, rows, sems, out_ref):
        def run(j, order):
            s = sets[j]

            def out(total):
                out_ref[:, LANES * j : LANES * (j + 1)] = total[: out_ref.shape[0]]

            if rows == 16:
                return direct_steps(pos, core, order, *s, sems, j * SCATTER_COPIES, out)
            return scatter_steps(pos, core, order, rows, s[0], s[1], s[2:6], s[6], s[7], s[8:12],
                                 s[12], s[13], sems, j * SCATTER_COPIES, out)

        return [run(j, order) for j, order in enumerate(ORDERS)]

    conv_sum = scatter(big, BLOCK, s_big, gconv_ref)
    advance(conv_sum)
    advance(weights)

    def unpack(g, _):
        y_lo, zz = lax.div(g, 4), lax.rem(g, 4)
        for i in range(16):
            at = {"x": i % 4, "y": 2 * ((i // 4) % 2) + y_lo, "z": zz}
            for j, (a, b, c) in enumerate(ORDERS):
                block = bufs[j][i // 8, at[a], at[b], at[c]].astype(jnp.float32)
                wide[81 * i : 81 * i + 81, LANES * j : LANES * (j + 1)] = block[:81]
        full[pl.ds(pl.multiple_of(g * 1296, 16), 1296)] = wide[...].astype(jnp.bfloat16)
        return 0

    lax.fori_loop(0, 8, unpack, 0)
    advance(conv_sum)

    def back(n, acc):
        rows, kernels = [], []
        for e in range(3):
            k = 3 * n + e
            m = 26 - k
            rows.append(g_taps[lax.rem(m, 9), pl.ds(pl.multiple_of(16 * lax.div(m, 9), 16), PIXELS), :])
            kernels.append(full[pl.ds(pl.multiple_of(k * CHANS, CHANS), CHANS), :])
        return acc + dot(jnp.concatenate(rows, 1), jnp.concatenate(kernels, 1), (1, 1))

    def ahead_conv(n, acc):
        rows = []
        for e in range(3):
            k = 3 * n + e
            rows.append(a_taps[lax.rem(k, 9), pl.ds(pl.multiple_of(16 * lax.div(k, 9), 16), PIXELS), :])
        kernel = full[pl.ds(pl.multiple_of(n * 3 * CHANS, CHANS), 3 * CHANS), :]
        return acc + dot(jnp.concatenate(rows, 1), kernel)

    acc = jnp.zeros((PIXELS, CHANS), jnp.float32)
    acc = lax.fori_loop(0, 3, back, acc)
    advance(conv_sum)
    acc = lax.fori_loop(3, 6, back, acc)
    advance(conv_sum)
    acc = lax.fori_loop(6, 9, back, acc)
    xhat = act32[...]
    z = xhat * gain + shift
    sigma = 1.0 / (1.0 + jnp.exp(-z))
    pre = acc * (sigma * (1.0 + z * (1.0 - sigma)))
    wide_pre = gbuf.at[pl.ds(0, PIXELS)]
    wide_pre[...] = pre
    total2 = []
    sums2 = sum_steps(f, r, sum_rows(pre, pre * xhat), total2.append, row2, frame2, s_sum2)
    next(sums2)
    acc = lax.fori_loop(0, 3, ahead_conv, jnp.zeros((PIXELS, CHANS), jnp.float32))
    next(sums2)
    advance(conv_sum)
    acc = lax.fori_loop(3, 5, ahead_conv, acc)
    next(sums2, None)
    gshift_ref[...] = total2[0][0:1].reshape(CHANS)
    ggain_ref[...] = total2[0][1:2].reshape(CHANS)
    means = group_sum(total2[0] * gain, mask[...]) / TALLY
    grown = rstd * (wide_pre[...] * gain - means[0:1] - act32[...] * means[1:2]) + grad32[...]
    l_out[0:16] = grown.reshape(16, 16, CHANS).astype(jnp.bfloat16)
    l_out[16] = jnp.zeros((16, CHANS), jnp.bfloat16)
    l_in[f] = l_out[pl.ds(f, 2)]
    lat_ops = spread_start(f, r, l_out, l_in, 2, s_lat)
    waiting += lat_ops
    advance(conv_sum)
    acc = lax.fori_loop(5, 9, ahead_conv, acc)
    code = acc + d_in[...].astype(jnp.float32).reshape(PIXELS, CHANS)
    code_ref[...] = code.reshape(16, 16, CHANS).astype(jnp.bfloat16)
    for op in lat_ops:
        op.wait_recv()
    got = l_in[...].astype(jnp.float32)

    def by_rows(block):
        return jnp.concatenate([block[:, :8].reshape(128, CHANS), block[:, 8:].reshape(128, CHANS)],
                               0).astype(jnp.bfloat16)

    lat, after = by_rows(got[:, 0]), by_rows(got[:, 1])
    thin = gbuf.at[pl.ds(0, 3 * CHANS)]
    thin[0:CHANS, :] = only(f > 0, dot(before[...].reshape(PIXELS, CHANS), lat, (0, 0)))
    thin[CHANS : 2 * CHANS, :] = dot(video[0].reshape(PIXELS, CHANS), lat, (0, 0))
    thin[2 * CHANS :, :] = dot(video[1].reshape(PIXELS, CHANS), lat, (0, 0))
    pack_rows(thin, 0, 8, 0, 9, 16, [s[0] for s in small])
    down_sum = scatter(small, 16, s_small, gdown_ref)
    advance(down_sum)
    advance(conv_sum)
    advance(down_sum)
    even = dot(lat, wd[CHANS : 2 * CHANS, :], (1, 1))
    odd = dot(lat, wd[2 * CHANS :, :], (1, 1)) + dot(after, wd[:CHANS, :], (1, 1))
    gvideo_ref[0] = even.reshape(2, 128, CHANS).astype(jnp.bfloat16)
    gvideo_ref[1] = odd.reshape(2, 128, CHANS).astype(jnp.bfloat16)
    advance(down_sum)
    advance(conv_sum)
    interleave(down_sum + conv_sum)
    for op in waiting:
        op.wait_send()


def hand_out(*refs):
    for source, target in zip(refs[:6], refs[6:]):
        target[...] = source[...]


def body(video, down_weight, conv_weight, norm_gain_vector, norm_shift_vector, output_gradient):
    vmem = pl.BlockSpec(memory_space=pltpu.VMEM)
    anywhere = pl.BlockSpec(memory_space=pl.ANY)
    bf16, f32 = jnp.bfloat16, jnp.float32

    def sems(count):
        return [pltpu.SemaphoreType.DMA((count,)), pltpu.SemaphoreType.DMA((count,))]

    buf = pltpu.VMEM((2, 4, 4, 4, BLOCK, LANES), bf16)
    rows = pltpu.VMEM((384, CHANS), bf16)
    scratch = [buf] * 3 + scatter_scratch(BLOCK) * 3 + direct_scratch(16) * 3 + [
        pltpu.VMEM((27 * CHANS, CHANS), bf16),
        pltpu.VMEM((8 * CHANS, CHANS), f32),
        pltpu.VMEM((1296, CHANS), f32),
        pltpu.VMEM((9, 288, CHANS), bf16),
        pltpu.VMEM((9, 288, CHANS), bf16),
        pltpu.VMEM((9, 512, LANES), f32),
        pltpu.VMEM((3, 64, LANES), f32),
        pltpu.VMEM((3, PIXELS, LANES), f32),
        rows, rows, rows, rows,
        pltpu.VMEM((2, 128, CHANS), bf16),
        pltpu.VMEM((16, 16, CHANS), bf16),
        pltpu.VMEM((16, 16, CHANS), bf16),
        pltpu.VMEM((17, 16, CHANS), bf16),
        pltpu.VMEM((16, 2, 16, CHANS), bf16),
        pltpu.VMEM((8, 8, CHANS), f32),
        pltpu.VMEM((16, 8, CHANS), f32),
        pltpu.VMEM((8, 8, CHANS), f32),
        pltpu.VMEM((16, 8, CHANS), f32),
        pltpu.VMEM((PIXELS, CHANS), f32),
        pltpu.VMEM((PIXELS, CHANS), f32),
        pltpu.VMEM((CHANS, CHANS), f32),
        pltpu.VMEM((2, 2, 128, CHANS), bf16),
        pltpu.VMEM((3 * CHANS, CHANS), bf16),
        pltpu.VMEM((81, CHANS), bf16),
        pltpu.VMEM((16, 16, CHANS), bf16),
        pltpu.SemaphoreType.DMA((4,)),
    ]
    scratch += sems(60) + sems(60) + sems(60) + sems(22) + sems(22) + sems(15) + sems(15)
    scratch += sems(8) + sems(8) + sems(1)
    results = pl.pallas_call(
        section_kernel,
        out_shape=(
            jax.ShapeDtypeStruct((16, 16, CHANS), bf16),
            jax.ShapeDtypeStruct((2, 2, 128, CHANS), bf16),
            jax.ShapeDtypeStruct((81, CHANS), f32),
            jax.ShapeDtypeStruct((9, CHANS), f32),
            jax.ShapeDtypeStruct((CHANS,), f32),
            jax.ShapeDtypeStruct((CHANS,), f32),
        ),
        in_specs=[anywhere] * 3 + [vmem] * 2 + [anywhere],
        out_specs=(vmem,) * 6,
        scratch_shapes=scratch,
        compiler_params=pltpu.CompilerParams(
            collective_id=0, has_side_effects=True, vmem_limit_bytes=63 * 2**20),
    )(video, down_weight, conv_weight, norm_gain_vector, norm_shift_vector,
      output_gradient.reshape(16, 16, CHANS))
    code, gvideo, gconv, gdown, ggain, gshift = pl.pallas_call(
        hand_out,
        out_shape=tuple(jax.ShapeDtypeStruct(x.shape, x.dtype) for x in results),
        in_specs=[vmem] * 6,
        out_specs=(vmem,) * 6,
    )(*results)
    return (code.reshape(16, 2, 8, CHANS), gvideo, gconv, gdown, ggain, gshift)


def solution(mesh):
    return jax.shard_map(
        body,
        mesh=mesh,
        in_specs=(
            P("frame", "row", None, None),
            P(),
            P(("frame", "row"), None),
            P(),
            P(),
            P(None, "row", "frame", None),
        ),
        out_specs=(
            P(None, "row", "frame", None),
            P("frame", "row", None, None),
            P(("frame", "row"), None),
            P(("frame", "row"), None),
            P(),
            P(),
        ),
        check_vma=False,
    )
```
